128 devices in a mesh: gx: 16 (over y, z), gy: 8 (over x, core).
Axes of the slice: x: 4, y: 4, z: 4, core: 2. Of those that a mesh axis runs over, the one named last changes fastest.
Arguments:
- feats: bfloat16 [16, 8, 16, 512, 128], P('gx', 'gy'), may hold values from -6 to 6
- voxel_mask: int32 [16, 8, 16, 512], P('gx', 'gy'), may hold values 0 or 1
- brick_coord: int32 [16, 8, 16, 3], P('gx', 'gy'), may hold values from 0 to 3, as said below
- brick_count: int32 [16, 8, 2], P('gx', 'gy'), may hold values from 5 to 8, as said below
- route: int32 [16, 8, 16, 2], P('gx', 'gy'), may hold values from 0 to 15, as said below
- conv_weight: bfloat16 [3456, 128], replicated, may hold values from -0.109375 to 0.109375
- down_weight: bfloat16 [1024, 128], replicated, may hold values from -0.1875 to 0.1875
- coarse_grad: bfloat16 [16, 8, 32, 64, 128], P('gx', 'gy'), may hold values from -24 to 24
Outputs:
- coarse: bfloat16 [16, 8, 32, 64, 128], P('gx', 'gy')
- feat_grad: bfloat16 [16, 8, 16, 512, 128], P('gx', 'gy')
- conv_grad: float32 [3456, 128], replicated
- down_grad: float32 [1024, 128], replicated
The draws below stay inside these ranges and needn't reach their ends.
Inputs may be any that keep to these rules, and one draw needn't show every extreme that they name: `brick_coord`: each slot names a brick position inside its device's tile of 4 x 4 x 4 bricks. The first 8 slots of a device hold distinct positions in the tile's outer brick columns (x or y equal to 0 or 3); the other slots hold distinct positions in the inner columns. `brick_count`: occupied slots come first in each half; some device has all its slots occupied. `route`: all slots of one device have distinct pairs (owner, place), so a device sends at most 2 sub-bricks to one owner; in every gy row one owner receives 2 sub-bricks from every device of the row.
All inputs are finite; a program needn't handle non-finite values. No bound on the sum of `voxel_mask` on one device may be relied on, other than what follows from the above.
Results may differ from the reference program's by a relative error of at most 0.005.
Values may be sent and summed in bfloat16 or wider, within the bound.
No kernel may reach another device: no remote copies, remote signals or barrier semaphores. Data moves between devices by JAX's collectives and lax.ppermute only.
A program may use at most 256 MiB of HBM per device.

```python
import math
import jax
import jax.numpy as jnp
import numpy as np
from jax import lax

CH = 128
EDGE = 8
VOX = 512
TILE = 4
DEPTH = 4
SLOTS = 16
BORDER = 8
CAP = 2
TILES_X = 16
TILES_Y = 8
RECV = 32


def outer_cells():
    found = [(x, y, z) for x in range(TILE) for y in range(TILE) for z in range(DEPTH) if x == 0 or y == 0 or x == TILE - 1 or (y == TILE - 1)]
    return np.array(found, dtype=np.int32)


def inner_cells():
    found = [(x, y, z) for x in range(1, TILE - 1) for y in range(1, TILE - 1) for z in range(DEPTH)]
    return np.array(found, dtype=np.int32)


def draw_brick_coord(key, part):
    key = jax.random.fold_in(key, 11)
    outer = jnp.asarray(outer_cells())
    inner = jnp.asarray(inner_cells())
    devices_total = TILES_X * TILES_Y
    keys_outer = jax.random.split(jax.random.fold_in(key, 1), devices_total)
    keys_inner = jax.random.split(jax.random.fold_in(key, 2), devices_total)
    pick_outer = jax.vmap(lambda k: jax.random.permutation(k, outer.shape[0])[:BORDER])(keys_outer)
    pick_inner = jax.vmap(lambda k: jax.random.permutation(k, inner.shape[0])[:BORDER])(keys_inner)
    coords = jnp.concatenate([outer[pick_outer], inner[pick_inner]], axis=1)
    return coords.reshape(TILES_X, TILES_Y, SLOTS, 3).astype(jnp.int32)


def draw_brick_count(key, part):
    key = jax.random.fold_in(key, 12)
    devices_total = TILES_X * TILES_Y
    lowest = max(1, BORDER - 3)
    counts = jax.random.randint(jax.random.fold_in(key, 1), (devices_total, 2), lowest, BORDER + 1)
    chosen = jax.random.randint(jax.random.fold_in(key, 2), (), 0, devices_total)
    filled = jnp.arange(devices_total, dtype=jnp.int32)[:, None] == chosen
    counts = jnp.where(filled, BORDER, counts)
    return counts.reshape(TILES_X, TILES_Y, 2).astype(jnp.int32)


def draw_route(key, part):
    key = jax.random.fold_in(key, 13)
    busy = jax.random.randint(jax.random.fold_in(key, 1), (TILES_Y,), 0, TILES_X).astype(jnp.int32)
    spare = (TILES_X - 1) * CAP
    keys_all = jax.random.split(jax.random.fold_in(key, 2), TILES_X * TILES_Y)
    picks = jax.vmap(lambda k: jax.random.permutation(k, spare)[:SLOTS - 2])(keys_all)
    picks = picks.reshape(TILES_X, TILES_Y, SLOTS - 2).astype(jnp.int32)
    hot = busy[None, :, None]
    other_owner = picks // CAP
    other_owner = other_owner + (other_owner >= hot).astype(jnp.int32)
    other_place = picks % CAP
    rest_slots = np.array([s for s in range(SLOTS) if s != 0 and s != BORDER], dtype=np.int32)
    owner = jnp.zeros((TILES_X, TILES_Y, SLOTS), jnp.int32)
    place = jnp.zeros((TILES_X, TILES_Y, SLOTS), jnp.int32)
    owner = owner.at[:, :, rest_slots].set(other_owner)
    place = place.at[:, :, rest_slots].set(other_place)
    busy_plane = jnp.broadcast_to(busy[None, :], (TILES_X, TILES_Y))
    owner = owner.at[:, :, 0].set(busy_plane).at[:, :, BORDER].set(busy_plane)
    place = place.at[:, :, 0].set(0).at[:, :, BORDER].set(1)
    return jnp.stack([owner, place], axis=-1).astype(jnp.int32)


def touch_ends(drawn, key, smallest, largest):
    shape = drawn.shape
    spot = [jax.random.randint(jax.random.fold_in(key, axis), (), 0, shape[axis]) for axis in range(len(shape))]
    drawn = drawn.at[tuple(spot)].set(smallest)
    longest = shape.index(max(shape))
    spot[longest] = (spot[longest] + 1) % shape[longest]
    return drawn.at[tuple(spot)].set(largest)


def steps_of(key, shape, cuts, least, high):
    gain = 1.0
    for axis_at, blocks in cuts:
        heights = jax.random.uniform(jax.random.fold_in(jax.random.fold_in(key, 6), axis_at), (blocks,), jnp.float32, least / len(cuts), high / len(cuts))
        gain = gain * jnp.repeat(jnp.exp(heights), shape[axis_at] // blocks).reshape((-1,) + (1,) * (len(shape) - 1 - axis_at))
    return gain


def noise(stream_key, dims, deviation, most, shards=(), held_as=jnp.bfloat16):
    drawn = deviation * jax.random.normal(stream_key, dims, jnp.float32)
    if shards:
        drawn = drawn * steps_of(stream_key, dims, shards, -0.22, 0.18)
    return jnp.clip(drawn, -most, most).astype(held_as)


def setup_inputs(seed: int = 0) -> dict:
    key_list = jax.random.split(jax.random.key(seed), 9)
    return {
        "feats": noise(key_list[0], (TILES_X, TILES_Y, SLOTS, VOX, CH), 1.0, 6.0, ((0, 16), (1, 8))),
        "voxel_mask": touch_ends((jax.random.randint(key_list[1], (TILES_X, TILES_Y, SLOTS, VOX), 0, 4) < 3).astype(jnp.int32), jax.random.fold_in(key_list[1], 1), 0, 1),
        "brick_coord": draw_brick_coord(jax.random.fold_in(key_list[8], 71), 0),
        "brick_count": draw_brick_count(jax.random.fold_in(key_list[8], 71), 0),
        "route": draw_route(jax.random.fold_in(key_list[8], 71), 0),
        "conv_weight": noise(key_list[5], (27 * CH, CH), (27 * CH) ** -0.5, 0.109375),
        "down_weight": noise(key_list[6], (8 * CH, CH), (8 * CH) ** -0.5, 0.1875),
        "coarse_grad": noise(key_list[7], (TILES_X, TILES_Y, RECV, VOX // 8, CH), 4.0, 24.0, ((0, 16), (1, 8))),
    }


def tap_offsets():
    return np.array([[a - 1, b - 1, c - 1] for a in range(3) for b in range(3) for c in range(3)], dtype=np.int32)

def unfold_taps(brick_pool, neighbour_index):
    edge = EDGE
    width = brick_pool.shape[-1]
    nearby = jnp.take(brick_pool, neighbour_index, axis=0)
    nearby = nearby.reshape(3, 3, 3, edge, edge, edge, width)
    nearby = nearby.transpose(0, 3, 1, 4, 2, 5, 6).reshape(3 * edge, 3 * edge, 3 * edge, width)
    padded = nearby[edge - 1:2 * edge + 1, edge - 1:2 * edge + 1, edge - 1:2 * edge + 1]
    columns = [padded[a:a + edge, b:b + edge, c:c + edge] for a in range(3) for b in range(3) for c in range(3)]
    return jnp.stack(columns, axis=3).reshape(edge ** 3, 27 * width)

def pool_pairs(activated):
    count = activated.shape[0]
    half = EDGE // 2
    blocks = activated.reshape(count, half, 2, half, 2, half, 2, CH).transpose(0, 1, 3, 5, 2, 4, 6, 7)
    return blocks.reshape(count * half ** 3, 8 * CH)

def unpool_pairs(columns, count):
    half = EDGE // 2
    blocks = columns.reshape(count, half, half, half, 2, 2, 2, CH).transpose(0, 1, 4, 2, 5, 3, 6, 7)
    return blocks.reshape(count, VOX, CH)

def reference(feats, voxel_mask, brick_coord, brick_count, route, conv_weight, down_weight, coarse_grad):
    tiles_x = TILES_X
    tiles_y = TILES_Y
    total_slots = tiles_x * tiles_y * SLOTS
    quarter = VOX // 8
    slot_ids = jnp.arange(SLOTS, dtype=jnp.int32)
    occupied = jnp.where(slot_ids < BORDER, slot_ids < brick_count[:, :, 0:1], slot_ids - BORDER < brick_count[:, :, 1:2])
    active = voxel_mask.astype(jnp.float32) * occupied.astype(jnp.float32)[..., None]
    inputs = feats * active.astype(jnp.bfloat16)[..., None]
    tile_i = jnp.arange(tiles_x, dtype=jnp.int32)[:, None, None]
    tile_j = jnp.arange(tiles_y, dtype=jnp.int32)[None, :, None]
    glob_x = brick_coord[..., 0] + TILE * tile_i
    glob_y = brick_coord[..., 1] + TILE * tile_j
    glob_z = brick_coord[..., 2]
    span_y = TILE * tiles_y + 2
    span_z = DEPTH + 2
    cells = (TILE * tiles_x + 2) * span_y * span_z
    position = ((glob_x + 1) * span_y + glob_y + 1) * span_z + glob_z + 1
    position = jnp.where(occupied, position, cells).reshape(-1).astype(jnp.int32)
    lookup = jnp.full((cells + 1,), total_slots, jnp.int32).at[position].set(jnp.arange(total_slots, dtype=jnp.int32))
    offsets = jnp.asarray(tap_offsets())
    flat_x = glob_x.reshape(-1, 1)
    flat_y = glob_y.reshape(-1, 1)
    flat_z = glob_z.reshape(-1, 1)
    wanted = ((flat_x + 1 + offsets[:, 0]) * span_y + flat_y + 1 + offsets[:, 1]) * span_z + flat_z + 1 + offsets[:, 2]
    neighbour_index = lookup[wanted.astype(jnp.int32)]
    empty_brick = jnp.zeros((1, VOX, CH), jnp.bfloat16)
    brick_pool = jnp.concatenate([inputs.reshape(total_slots, VOX, CH), empty_brick], axis=0)
    flat_active = active.reshape(total_slots, VOX)

    def forward_one(row_index):
        return jnp.dot(unfold_taps(brick_pool, row_index), conv_weight, preferred_element_type=jnp.float32)
    preact = lax.map(forward_one, neighbour_index)
    activated = (jax.nn.silu(preact) * flat_active[..., None]).astype(jnp.bfloat16)
    block_rows = pool_pairs(activated)
    sub_rows = jnp.dot(block_rows, down_weight, preferred_element_type=jnp.float32).astype(jnp.bfloat16)
    received_count = CAP * tiles_x
    owner = route[..., 0]
    place = route[..., 1]
    target = (owner * tiles_y + tile_j) * received_count + tile_i * CAP + place
    dump = tiles_x * tiles_y * received_count
    target = jnp.where(occupied, target, dump).reshape(-1).astype(jnp.int32)
    coarse = jnp.zeros((dump + 1, quarter, CH), jnp.bfloat16).at[target].set(sub_rows.reshape(total_slots, quarter, CH))
    coarse = coarse[:dump].reshape(tiles_x, tiles_y, received_count, quarter, CH)
    grad_flat = jnp.concatenate([coarse_grad.reshape(dump, quarter, CH), jnp.zeros((1, quarter, CH), jnp.bfloat16)], axis=0)
    grad_rows = grad_flat[target].reshape(total_slots * quarter, CH)
    down_grad = lax.dot_general(block_rows, grad_rows, (((0,), (0,)), ((), ())), preferred_element_type=jnp.float32)
    back_rows = jnp.dot(grad_rows, down_weight.T, preferred_element_type=jnp.float32)
    grad_act = unpool_pairs(back_rows, total_slots)
    sigmoid_z = jax.nn.sigmoid(preact)
    grad_pre = (grad_act * flat_active[..., None] * sigmoid_z * (1.0 + preact * (1.0 - sigmoid_z))).astype(jnp.bfloat16)
    grad_pool = jnp.concatenate([grad_pre, empty_brick], axis=0)
    flipped = conv_weight.reshape(27, CH, CH)[::-1].transpose(0, 2, 1).reshape(27 * CH, CH)

    def backward_one(running, item):
        row_index, grad_slot = item
        running = running + lax.dot_general(unfold_taps(brick_pool, row_index), grad_slot, (((0,), (0,)), ((), ())), preferred_element_type=jnp.float32)
        back = jnp.dot(unfold_taps(grad_pool, row_index), flipped, preferred_element_type=jnp.float32)
        return (running, back)
    conv_grad, back_all = lax.scan(backward_one, jnp.zeros((27 * CH, CH), jnp.float32), (neighbour_index, grad_pre))
    feat_grad = (back_all * flat_active[..., None]).astype(jnp.bfloat16).reshape(feats.shape)
    conv_grad = conv_grad * (1.0 / math.sqrt(total_slots * VOX))
    down_grad = down_grad * (1.0 / math.sqrt(total_slots * VOX // 8))
    return (coarse, feat_grad, conv_grad, down_grad)
```

```python
import math

import jax
import jax.numpy as jnp
import numpy as np
from jax import lax
from jax.experimental import pallas as pl
from jax.experimental.pallas import tpu as pltpu
from jax.sharding import PartitionSpec as P

CH = 128
EDGE = 8
VOX = 512
TILE = 4
SLOTS = 16
BORDER = 8
CAP = 2
BF = jnp.bfloat16
F32 = jnp.float32
FACE = 64 * BORDER
LAB = 16
XMSG = FACE + LAB
YMSG = XMSG + 2 * 64 + 2 * LAB
SHARD = 40
VSTEP = 4096
NOWHERE = -(1 << 20)


def position_code(x, y, z):
    return (x + TILE) * 96 + (y + TILE) * 8 + z + 1


def label_code(row, shift_x, shift_y):
    packed = row.astype(F32).astype(jnp.int32) - 1
    code = position_code(
        (packed & 3) + shift_x * TILE, ((packed >> 2) & 3) + shift_y * TILE, packed >> 4
    )
    return jnp.where(packed < 0, NOWHERE, code)


def one_hot(left, right):
    return jnp.where(left == right, 1.0, 0.0).astype(BF)


def tap_delta(a, b, c):
    return (a - 1) * 96 + (b - 1) * 8 + (c - 1)


def lane_row():
    return lax.broadcasted_iota(jnp.int32, (1, 128), 1)


def tile_at(vol, xp, yp, zp):
    return vol[xp, yp, zp // 2, :, (zp % 2) * CH : (zp % 2 + 1) * CH]


def put_tile(vol, xp, yp, zp, value):
    vol[xp, yp, zp // 2, :, (zp % 2) * CH : (zp % 2 + 1) * CH] = value


def fill_halo(vol, sel, meta, left, right, lower, upper):
    base = meta[0:SLOTS]
    lane = lane_row()
    own = meta[2 * SLOTS : 2 * SLOTS + 1] + VSTEP * (lane // SLOTS)
    nothing = jnp.zeros((SLOTS, 128), BF)
    zs = [7, 0, 1, 2, 3, 4, 5, 6, 7, 0]
    cs = [0] + [1] * 8 + [2]

    sides = [
        (0, 1, left, -1, 0),
        (2, 1, right, 1, 0),
        (1, 0, lower, 0, -1),
        (1, 2, upper, 0, 1),
    ]
    for a, b, msg, sx, sy in sides:
        far = label_code(msg[FACE : FACE + 1], sx, sy) + VSTEP * (lane // BORDER)
        for zp in range(10):
            for col in range(2):
                rows = pl.ds((zp * 2 + col) * SLOTS, SLOTS)
                want = base + (tap_delta(a, b, cs[zp]) + VSTEP * (col * 8 + zs[zp]))
                here = one_hot(want, own + VSTEP * 8 * col)
                sel[rows, col * 128 : (col + 1) * 128] = here
                sel[rows, (1 - col) * 128 : (2 - col) * 128] = nothing
                sel[rows, 256:384] = one_hot(want, far)
        for half in range(2):
            parts = []
            for k in range(2):
                first = (half * 2 + k) * 2
                tiles = []
                for col in range(2):
                    for z in range(8):
                        if b == 1:
                            tiles.append(tile_at(vol, 8 if a == 0 else 1, first + col + 1, z + 1))
                        else:
                            tiles.append(tile_at(vol, first + col + 1, 8 if b == 0 else 1, z + 1))
                tiles.append(msg[first * 64 : (first + 2) * 64])
                parts.append(jnp.concatenate(tiles, axis=0))
            data = jnp.concatenate(parts, axis=1)
            out = jnp.dot(sel[0:320, :], data, preferred_element_type=F32).astype(BF)
            for k in range(2):
                for zp in range(10):
                    for col in range(2):
                        at = (half * 2 + k) * 2 + col + 1
                        row = (zp * 2 + col) * SLOTS
                        value = out[row : row + SLOTS, k * 128 : (k + 1) * 128]
                        if b == 1:
                            put_tile(vol, 0 if a == 0 else 9, at, zp, value)
                        else:
                            put_tile(vol, at, 0 if b == 0 else 9, zp, value)

    for c in (0, 2):
        for v in range(16):
            rows = pl.ds(v * SLOTS, SLOTS)
            j = v // 8
            want = base + (tap_delta(1, 1, c) + VSTEP * v)
            sel[rows, j * 128 : (j + 1) * 128] = one_hot(want, own + VSTEP * 8 * j)
            sel[rows, (1 - j) * 128 : (2 - j) * 128] = nothing
        for half in range(2):
            parts = []
            for k in range(2):
                tiles = []
                for v in range(16):
                    at = (half * 2 + k) * 16 + v
                    tiles.append(tile_at(vol, at // 8 + 1, at % 8 + 1, 8 if c == 0 else 1))
                parts.append(jnp.concatenate(tiles, axis=0))
            data = jnp.concatenate(parts, axis=1)
            out = jnp.dot(sel[0:256, 0:256], data, preferred_element_type=F32).astype(BF)
            for k in range(2):
                for v in range(16):
                    at = (half * 2 + k) * 16 + v
                    put_tile(
                        vol,
                        at // 8 + 1,
                        at % 8 + 1,
                        0 if c == 0 else 9,
                        out[v * SLOTS : (v + 1) * SLOTS, k * 128 : (k + 1) * 128],
                    )

    for a in (0, 2):
        for b in (0, 2):
            side = left if a == 0 else right
            face = lower if b == 0 else upper
            side_code = label_code(side[FACE : FACE + 1], a - 1, 0)
            face_code = label_code(face[FACE : FACE + 1], 0, b - 1)
            corner_at = XMSG if a == 0 else XMSG + 64
            corner_lab = XMSG + 128 if a == 0 else XMSG + 128 + LAB
            corner_code = label_code(face[corner_lab : corner_lab + 1], a - 1, b - 1)
            voxel = VSTEP * (lane % 64 // BORDER)
            beside = jnp.where(lane < 64, side_code, face_code) + voxel
            across = jnp.where(lane < 64, corner_code, NOWHERE) + voxel
            for zp in range(10):
                rows = pl.ds(zp * SLOTS, SLOTS)
                want = base + (tap_delta(a, b, cs[zp]) + VSTEP * zs[zp])
                sel[rows, 0:128] = one_hot(want, own)
                sel[rows, 128:256] = one_hot(want, beside)
                sel[rows, 256:384] = one_hot(want, across)
            xs = 8 if a == 0 else 1
            ys = 8 if b == 0 else 1
            tiles = [tile_at(vol, xs, ys, z + 1) for z in range(8)]
            line_y = (7 if b == 0 else 0) * 64
            line_x = (7 if a == 0 else 0) * 64
            tiles.append(side[line_y : line_y + 64])
            tiles.append(face[line_x : line_x + 64])
            tiles.append(face[corner_at : corner_at + 64])
            tiles.append(jnp.zeros((64, CH), BF))
            data = jnp.concatenate(tiles, axis=0)
            out = jnp.dot(sel[0:160, :], data, preferred_element_type=F32).astype(BF)
            for zp in range(10):
                put_tile(
                    vol,
                    0 if a == 0 else 9,
                    0 if b == 0 else 9,
                    zp,
                    out[zp * SLOTS : (zp + 1) * SLOTS],
                )


def pair_weights(wide, block):
    zero = jnp.zeros((CH, CH), BF)
    for a in range(3):
        for b in range(3):
            w0, w1, w2 = (block(a, b, c) for c in range(3))
            k = (a * 3 + b) * 2
            wide[k * 256 : k * 256 + 128, 0:128] = w0
            wide[k * 256 : k * 256 + 128, 128:256] = zero
            wide[k * 256 + 128 : k * 256 + 256, 0:128] = w1
            wide[k * 256 + 128 : k * 256 + 256, 128:256] = w0
            wide[k * 256 + 256 : k * 256 + 384, 0:128] = w2
            wide[k * 256 + 256 : k * 256 + 384, 128:256] = w1
            wide[k * 256 + 384 : k * 256 + 512, 0:128] = zero
            wide[k * 256 + 384 : k * 256 + 512, 128:256] = w2


def window(vol, x0, nx, a, b, h):
    return vol[pl.ds(x0 + a, nx), b : b + EDGE, h : h + 4].reshape(nx * EDGE * 4 * SLOTS, 256)


def conv_rows(vol, wide, x0, nx):
    taps = [window(vol, x0, nx, k // 6, k // 2 % 3, k % 2) for k in range(18)]
    return jnp.dot(jnp.concatenate(taps, axis=1), wide[...], preferred_element_type=F32)


def arrange_kernel(feats, mask_rows, labels, vol, mask, xlo, xhi, ylo, yhi):
    r = lax.broadcasted_iota(jnp.int32, (256, 256), 0)
    k = lax.broadcasted_iota(jnp.int32, (256, 256), 1)
    order = one_hot((r % SLOTS) * 16 + r // SLOTS, k)
    ones = jnp.ones((256, CH), BF)

    def at_x(x, carry):
        for q in range(4):
            first = pl.multiple_of(x * 64 + q * 16, 16)
            data = feats[:, pl.ds(first, 16), :].reshape(256, CH)
            chosen = order * mask_rows[x, q : q + 1, :]
            out = jnp.dot(
                chosen, jnp.concatenate([data, ones], axis=1), preferred_element_type=F32
            )
            tiles = out.astype(BF).reshape(2, 8, SLOTS, 256)
            for y in range(2):
                for z in range(8):
                    put_tile(vol, x + 1, q * 2 + y + 1, z + 1, tiles[y, z, :, 0:CH])
                    mask[x, q * 2 + y, z // 2, :, (z % 2) * CH : (z % 2 + 1) * CH] = tiles[
                        y, z, :, CH : 2 * CH
                    ]
            outer = out[:, 0:CH].reshape(2, 8, SLOTS, CH)[:, :, 0:BORDER]

            @pl.when(x == 0)
            def _():
                xlo[q * 128 : (q + 1) * 128] = outer.reshape(128, CH).astype(BF)

            @pl.when(x == EDGE - 1)
            def _():
                xhi[q * 128 : (q + 1) * 128] = outer.reshape(128, CH).astype(BF)

            line = pl.ds(pl.multiple_of(x * 64, 64), 64)
            if q == 0:
                ylo[line] = outer[0].reshape(64, CH).astype(BF)
            if q == 3:
                yhi[line] = outer[1].reshape(64, CH).astype(BF)
        return carry

    lax.fori_loop(0, EDGE, at_x, 0)
    for face in (xlo, xhi, ylo, yhi):
        face[FACE:XMSG] = labels[...]


def forward_kernel(
    vol_in, mask, left, right, lower, upper, meta, weight, down, returned, labels,
    grad_vol, gxlo, gxhi, gylo, gyhi, sending, partial,
    vol, sel, wide, grad_t, route, spread, acts, subs,
):
    vol[...] = vol_in[...]
    pair_weights(wide, lambda a, b, c: weight[((a * 3 + b) * 3 + c) * CH :][:CH])
    fill_halo(vol, sel, meta, left, right, lower, upper)

    lane = lane_row()
    for b in range(16):
        for j in range(4):
            route[b * 16 : (b + 1) * 16, j * 128 : (j + 1) * 128] = one_hot(
                meta[SLOTS : 2 * SLOTS] * 16 + b, lane + 128 * j
            )
    block = lax.broadcasted_iota(jnp.int32, (16, 128), 0)
    for t in range(2 * SLOTS):
        for j in range(2):
            spread[t * 16 : (t + 1) * 16, j * 128 : (j + 1) * 128] = one_hot(
                block * 64 + t, meta[2 * SLOTS + 1 : 2 * SLOTS + 2] + 64 * (lane // 16 + 8 * j)
            )

    def at_hx(hx, carry):
        pre_all = conv_rows(vol, wide, 2 * hx, 2).reshape(2, 4, 2, 64, 256)
        first = pl.multiple_of(hx * 16, 16)
        grad_sub = jnp.dot(
            route[...],
            returned[:, pl.ds(first, 16), :].reshape(512, CH),
            preferred_element_type=F32,
        ).astype(BF)
        subs[pl.ds(pl.multiple_of(hx * 256, 256), 256)] = grad_sub
        grad_act = lax.dot_general(
            grad_sub, down[...], (((1,), (1,)), ((), ())), preferred_element_type=F32
        )
        total = None
        for px in range(2):
            for py in range(2):
                q = px * 2 + py
                x = 2 * hx + px
                pre = pre_all[px, :, py].reshape(256, 256)
                live = jnp.stack([mask[x, 2 * hy + py] for hy in range(4)]).reshape(256, 256)
                live = live.astype(F32)
                sig = jax.nn.sigmoid(pre)
                act = (pre * sig * live).astype(BF)
                acts[q, pl.ds(pl.multiple_of(hx * 256, 256), 256)] = act
                term = jnp.dot(
                    act, down[q * 256 : (q + 1) * 256], preferred_element_type=F32
                )
                total = term if total is None else total + term
                grad = (
                    grad_act[:, q * 256 : (q + 1) * 256]
                    * live
                    * sig
                    * (1.0 + pre * (1.0 - sig))
                )
                grad_b = grad.astype(BF)
                shaped = grad_b.reshape(4, 4, SLOTS, 256)
                outer = grad.reshape(4, 4, SLOTS, 256)[:, :, 0:BORDER]
                turned = grad_b.T
                for hy in range(4):
                    y = 2 * hy + py
                    for p in range(4):
                        put_tile(grad_vol, x + 1, y + 1, 2 * p + 1, shaped[hy, p, :, 0:CH])
                        put_tile(grad_vol, x + 1, y + 1, 2 * p + 2, shaped[hy, p, :, CH:256])
                    zs = jnp.stack(
                        [outer[hy, z // 2, :, (z % 2) * CH : (z % 2 + 1) * CH] for z in range(8)]
                    )
                    flat = zs.reshape(64, CH).astype(BF)
                    if px == 0:
                        @pl.when(hx == 0)
                        def _():
                            gxlo[y * 64 : (y + 1) * 64] = flat
                    else:
                        @pl.when(hx == 3)
                        def _():
                            gxhi[y * 64 : (y + 1) * 64] = flat
                    line = pl.ds(pl.multiple_of(x * 64, 64), 64)
                    if y == 0:
                        gylo[line] = flat
                    if y == EDGE - 1:
                        gyhi[line] = flat
                grad_t[hx, q] = turned
        sub = total.astype(BF)
        sent = jnp.dot(spread[...], sub, preferred_element_type=F32).astype(BF)
        sending[:, pl.ds(first, 16), :] = sent.reshape(2 * SLOTS, 16, CH)
        return carry

    lax.fori_loop(0, EDGE // 2, at_hx, 0)
    for face in (gxlo, gxhi, gylo, gyhi):
        face[FACE:XMSG] = labels[...]

    subs_t = subs[...].T
    for q in range(4):
        found = jnp.dot(subs_t, acts[q], preferred_element_type=F32)
        partial[3456 + q * 256 : 3456 + (q + 1) * 256] = found.T.astype(BF)

    def at_tap(ab, carry):
        a = ab // 3
        b = lax.rem(ab, 3)
        halves = []
        for h in range(2):
            total = None
            for hx in range(4):
                for q in range(4):
                    px, py = q // 2, q % 2
                    rows = jnp.stack(
                        [
                            vol[2 * hx + px + a, 2 * hy + py + b, h : h + 4]
                            for hy in range(4)
                        ]
                    ).reshape(256, 256)
                    term = jnp.dot(grad_t[hx, q], rows, preferred_element_type=F32)
                    total = term if total is None else total + term
            halves.append(total)
        low, high = halves
        taps = [
            low[0:128, 0:128] + low[128:256, 128:256],
            low[0:128, 128:256] + high[128:256, 0:128],
            high[0:128, 0:128] + high[128:256, 128:256],
        ]
        for c in range(3):
            row = pl.multiple_of((ab * 3 + c) * CH, CH)
            partial[pl.ds(row, CH)] = taps[c].T.astype(BF)
        return carry

    lax.fori_loop(0, 9, at_tap, 0)
    partial[4480:] = jnp.zeros((SHARD * 128 - 4480, CH), BF)


def backward_kernel(
    vol_in, mask_rows, left, right, lower, upper, meta, weight, feat_grad, vol, sel, wide
):
    vol[...] = vol_in[...]
    pair_weights(
        wide, lambda a, b, c: weight[((2 - a) * 9 + (2 - b) * 3 + 2 - c) * CH :][:CH].T
    )
    fill_halo(vol, sel, meta, left, right, lower, upper)
    r = lax.broadcasted_iota(jnp.int32, (256, 256), 0)
    k = lax.broadcasted_iota(jnp.int32, (256, 256), 1)
    order = one_hot(
        (r % 2) * 128 + (r // 8 % 2) * 64 + (r // 2 % 4) * 16 + r // 16, k
    )

    def at_hx(hx, carry):
        back = conv_rows(vol, wide, 2 * hx, 2).astype(BF).reshape(2, 4, 128, 256)
        for px in range(2):
            for q in range(4):
                x = 2 * hx + px
                data = jnp.concatenate(
                    [back[px, q, :, 0:CH], back[px, q, :, CH:256]], axis=0
                )
                chosen = order * mask_rows[x, q : q + 1, :]
                out = jnp.dot(chosen, data, preferred_element_type=F32).astype(BF)
                first = pl.multiple_of(x * 64 + q * 16, 16)
                feat_grad[:, pl.ds(first, 16), :] = out.reshape(SLOTS, 16, CH)
        return carry

    lax.fori_loop(0, EDGE // 2, at_hx, 0)


VMEM_LIMIT = 56 * 1024 * 1024
VOLUME = (10, 10, 5, SLOTS, 256)


def whole(count):
    return [pl.BlockSpec(memory_space=pltpu.VMEM)] * count


def shift(value, axis, step):
    count = lax.axis_size(axis)
    if step > 0:
        pairs = [(i, i + 1) for i in range(count - 1)]
    else:
        pairs = [(i + 1, i) for i in range(count - 1)]
    return lax.ppermute(value, axis, pairs)


def exchange(xlo, xhi, ylo, yhi):
    left = shift(xhi, "gx", 1)
    right = shift(xlo, "gx", -1)
    ends = [left[FACE:XMSG], right[FACE:XMSG]]
    up = jnp.concatenate([yhi, left[FACE - 64 : FACE], right[FACE - 64 : FACE]] + ends)
    down = jnp.concatenate([ylo, left[0:64], right[0:64]] + ends)
    lower = shift(up, "gy", 1)
    upper = shift(down, "gy", -1)
    return left, right, lower, upper


def per_device(
    feats, voxel_mask, brick_coord, brick_count, route, conv_weight, down_weight, coarse_grad
):
    tiles_x = lax.axis_size("gx")
    tiles_y = lax.axis_size("gy")
    devices = tiles_x * tiles_y
    slot_ids = jnp.arange(SLOTS, dtype=jnp.int32)
    counts = brick_count[0, 0]
    occupied = jnp.where(slot_ids < BORDER, slot_ids < counts[0], slot_ids - BORDER < counts[1])
    coords = brick_coord[0, 0]
    active = (voxel_mask[0, 0] * occupied.astype(jnp.int32)[:, None]).astype(BF)
    by_chunk = active.reshape(SLOTS, EDGE, 4, 16)
    mask_rows = by_chunk.transpose(1, 2, 0, 3).reshape(EDGE, 4, 256)
    by_pair = active.reshape(SLOTS, EDGE, 4, 2, 4, 2)
    back_rows = by_pair.transpose(1, 2, 5, 3, 4, 0).reshape(EDGE, 4, 256)
    packed = 1 + coords[:, 0] + TILE * coords[:, 1] + TILE * TILE * coords[:, 2]
    labels = jnp.where(occupied, packed, 0)[:BORDER]
    labels = jnp.broadcast_to(jnp.tile(labels, 128 // BORDER)[None], (LAB, 128)).astype(BF)
    own = position_code(coords[:, 0], coords[:, 1], coords[:, 2])
    target = jnp.where(occupied, route[0, 0, :, 0] * CAP + route[0, 0, :, 1], NOWHERE)
    meta = jnp.concatenate(
        [
            jnp.broadcast_to(own[:, None], (SLOTS, 128)),
            jnp.broadcast_to(target[:, None], (SLOTS, 128)),
            jnp.tile(jnp.where(occupied, own, NOWHERE), 8)[None],
            jnp.tile(target, 8)[None],
            jnp.zeros((6, 128), jnp.int32),
        ]
    )

    params = pltpu.CompilerParams(vmem_limit_bytes=VMEM_LIMIT)
    face = jax.ShapeDtypeStruct((XMSG, CH), BF)
    volume = jax.ShapeDtypeStruct(VOLUME, BF)
    vol, mask, xlo, xhi, ylo, yhi = pl.pallas_call(
        arrange_kernel,
        out_shape=(volume, jax.ShapeDtypeStruct((8, 8, 4, SLOTS, 256), BF)) + (face,) * 4,
        in_specs=whole(3),
        out_specs=tuple(whole(6)),
        compiler_params=params,
        name="arrange",
    )(feats[0, 0], mask_rows, labels)
    around = exchange(xlo, xhi, ylo, yhi)
    returned = lax.all_to_all(
        coarse_grad[0, 0].reshape(tiles_x, CAP * 64, CH), "gx", 0, 0, tiled=True
    ).reshape(2 * SLOTS, 64, CH)

    grad_vol, gxlo, gxhi, gylo, gyhi, sending, partial = pl.pallas_call(
        forward_kernel,
        out_shape=(volume,)
        + (face,) * 4
        + (
            jax.ShapeDtypeStruct((2 * SLOTS, 64, CH), BF),
            jax.ShapeDtypeStruct((SHARD * 128, CH), BF),
        ),
        in_specs=whole(11),
        out_specs=tuple(whole(7)),
        scratch_shapes=[
            pltpu.VMEM(VOLUME, BF),
            pltpu.VMEM((320, 384), BF),
            pltpu.VMEM((18 * 256, 256), BF),
            pltpu.VMEM((4, 4, 256, 256), BF),
            pltpu.VMEM((256, 512), BF),
            pltpu.VMEM((512, 256), BF),
            pltpu.VMEM((4, 1024, 256), BF),
            pltpu.VMEM((1024, CH), BF),
        ],
        compiler_params=params,
        name="forward",
    )(vol, mask, *around, meta, conv_weight, down_weight, returned, labels)

    parts = lax.all_to_all(
        partial.reshape(devices, SHARD, CH), ("gx", "gy"), 0, 0, tiled=True
    )
    around = exchange(gxlo, gxhi, gylo, gyhi)
    feat_grad = pl.pallas_call(
        backward_kernel,
        out_shape=jax.ShapeDtypeStruct((SLOTS, VOX, CH), BF),
        in_specs=whole(8),
        out_specs=whole(1)[0],
        scratch_shapes=[
            pltpu.VMEM(VOLUME, BF),
            pltpu.VMEM((320, 384), BF),
            pltpu.VMEM((18 * 256, 256), BF),
        ],
        compiler_params=params,
        name="backward",
    )(grad_vol, back_rows, *around, meta, conv_weight)

    total = jnp.sum(parts.astype(F32), axis=0).astype(BF)
    coarse = lax.all_to_all(
        sending.reshape(tiles_x, CAP * 64, CH), "gx", 0, 0, tiled=True
    ).reshape(1, 1, 2 * SLOTS, 64, CH)
    sums = lax.all_to_all(
        jnp.broadcast_to(total[None], (devices, SHARD, CH)), ("gx", "gy"), 0, 0, tiled=True
    ).reshape(devices * SHARD, CH)
    total_slots = devices * SLOTS
    conv_grad = sums[:3456].astype(F32) * (1.0 / math.sqrt(total_slots * VOX))
    down_grad = sums[3456:4480].astype(F32) * (1.0 / math.sqrt(total_slots * VOX // 8))
    return (coarse, feat_grad[None, None], conv_grad, down_grad)


def solution(mesh):
    in_specs = (
        P("gx", "gy", None, None, None),
        P("gx", "gy", None, None),
        P("gx", "gy", None, None),
        P("gx", "gy", None),
        P("gx", "gy", None, None),
        P(),
        P(),
        P("gx", "gy", None, None, None),
    )
    out_specs = (P("gx", "gy", None, None, None), P("gx", "gy", None, None, None), P(), P())
    return jax.shard_map(
        per_device, mesh=mesh, in_specs=in_specs, out_specs=out_specs, check_vma=False
    )
```

```python
import math

import jax
import jax.numpy as jnp
import numpy as np
from jax import lax
from jax.experimental import pallas as pl
from jax.experimental.pallas import tpu as pltpu
from jax.sharding import PartitionSpec as P

CH = 128
EDGE = 8
VOX = 512
TILE = 4
SLOTS = 16
BORDER = 8
CAP = 2
BF = jnp.bfloat16
F32 = jnp.float32
FACE = 64 * BORDER
LAB = 16
XMSG = FACE + LAB
YMSG = XMSG + 2 * 64 + 2 * LAB
SHARD = 40
VSTEP = 4096
NOWHERE = -(1 << 20)


def position_code(x, y, z):
    return (x + TILE) * 96 + (y + TILE) * 8 + z + 1


def label_code(row, shift_x, shift_y):
    packed = row.astype(F32).astype(jnp.int32) - 1
    code = position_code(
        (packed & 3) + shift_x * TILE, ((packed >> 2) & 3) + shift_y * TILE, packed >> 4
    )
    return jnp.where(packed < 0, NOWHERE, code)


def one_hot(left, right):
    return jnp.where(left == right, 1.0, 0.0).astype(BF)


def tap_delta(a, b, c):
    return (a - 1) * 96 + (b - 1) * 8 + (c - 1)


def lane_row():
    return lax.broadcasted_iota(jnp.int32, (1, 128), 1)


def tile_at(vol, xp, yp, zp):
    return vol[xp, yp, zp // 2, :, (zp % 2) * CH : (zp % 2 + 1) * CH]


def put_tile(vol, xp, yp, zp, value):
    vol[xp, yp, zp // 2, :, (zp % 2) * CH : (zp % 2 + 1) * CH] = value


def fill_halo(vol, sel, base, own, left, right, lower, upper):
    lane = lane_row()
    own = own + VSTEP * (lane // SLOTS)
    nothing = jnp.zeros((SLOTS, 128), BF)
    zs = [7, 0, 1, 2, 3, 4, 5, 6, 7, 0]
    cs = [0] + [1] * 8 + [2]

    sides = [
        (0, 1, left, -1, 0),
        (2, 1, right, 1, 0),
        (1, 0, lower, 0, -1),
        (1, 2, upper, 0, 1),
    ]
    for a, b, msg, sx, sy in sides:
        far = label_code(msg[FACE : FACE + 1], sx, sy) + VSTEP * (lane // BORDER)
        for zp in range(10):
            for col in range(2):
                rows = pl.ds((zp * 2 + col) * SLOTS, SLOTS)
                want = base + (tap_delta(a, b, cs[zp]) + VSTEP * (col * 8 + zs[zp]))
                here = one_hot(want, own + VSTEP * 8 * col)
                sel[rows, col * 128 : (col + 1) * 128] = here
                sel[rows, (1 - col) * 128 : (2 - col) * 128] = nothing
                sel[rows, 256:384] = one_hot(want, far)
        for half in range(2):
            parts = []
            for k in range(2):
                first = (half * 2 + k) * 2
                tiles = []
                for col in range(2):
                    for z in range(8):
                        if b == 1:
                            tiles.append(tile_at(vol, 8 if a == 0 else 1, first + col + 1, z + 1))
                        else:
                            tiles.append(tile_at(vol, first + col + 1, 8 if b == 0 else 1, z + 1))
                tiles.append(msg[first * 64 : (first + 2) * 64])
                parts.append(jnp.concatenate(tiles, axis=0))
            data = jnp.concatenate(parts, axis=1)
            out = jnp.dot(sel[0:320, :], data, preferred_element_type=F32).astype(BF)
            for k in range(2):
                for zp in range(10):
                    for col in range(2):
                        at = (half * 2 + k) * 2 + col + 1
                        row = (zp * 2 + col) * SLOTS
                        value = out[row : row + SLOTS, k * 128 : (k + 1) * 128]
                        if b == 1:
                            put_tile(vol, 0 if a == 0 else 9, at, zp, value)
                        else:
                            put_tile(vol, at, 0 if b == 0 else 9, zp, value)

    for c in (0, 2):
        for v in range(16):
            rows = pl.ds(v * SLOTS, SLOTS)
            j = v // 8
            want = base + (tap_delta(1, 1, c) + VSTEP * v)
            sel[rows, j * 128 : (j + 1) * 128] = one_hot(want, own + VSTEP * 8 * j)
            sel[rows, (1 - j) * 128 : (2 - j) * 128] = nothing
        for half in range(2):
            parts = []
            for k in range(2):
                tiles = []
                for v in range(16):
                    at = (half * 2 + k) * 16 + v
                    tiles.append(tile_at(vol, at // 8 + 1, at % 8 + 1, 8 if c == 0 else 1))
                parts.append(jnp.concatenate(tiles, axis=0))
            data = jnp.concatenate(parts, axis=1)
            out = jnp.dot(sel[0:256, 0:256], data, preferred_element_type=F32).astype(BF)
            for k in range(2):
                for v in range(16):
                    at = (half * 2 + k) * 16 + v
                    put_tile(
                        vol,
                        at // 8 + 1,
                        at % 8 + 1,
                        0 if c == 0 else 9,
                        out[v * SLOTS : (v + 1) * SLOTS, k * 128 : (k + 1) * 128],
                    )

    for a in (0, 2):
        for b in (0, 2):
            side = left if a == 0 else right
            face = lower if b == 0 else upper
            side_code = label_code(side[FACE : FACE + 1], a - 1, 0)
            face_code = label_code(face[FACE : FACE + 1], 0, b - 1)
            corner_at = XMSG if a == 0 else XMSG + 64
            corner_lab = XMSG + 128 if a == 0 else XMSG + 128 + LAB
            corner_code = label_code(face[corner_lab : corner_lab + 1], a - 1, b - 1)
            voxel = VSTEP * (lane % 64 // BORDER)
            beside = jnp.where(lane < 64, side_code, face_code) + voxel
            across = jnp.where(lane < 64, corner_code, NOWHERE) + voxel
            for zp in range(10):
                rows = pl.ds(zp * SLOTS, SLOTS)
                want = base + (tap_delta(a, b, cs[zp]) + VSTEP * zs[zp])
                sel[rows, 0:128] = one_hot(want, own)
                sel[rows, 128:256] = one_hot(want, beside)
                sel[rows, 256:384] = one_hot(want, across)
            xs = 8 if a == 0 else 1
            ys = 8 if b == 0 else 1
            tiles = [tile_at(vol, xs, ys, z + 1) for z in range(8)]
            line_y = (7 if b == 0 else 0) * 64
            line_x = (7 if a == 0 else 0) * 64
            tiles.append(side[line_y : line_y + 64])
            tiles.append(face[line_x : line_x + 64])
            tiles.append(face[corner_at : corner_at + 64])
            tiles.append(jnp.zeros((64, CH), BF))
            data = jnp.concatenate(tiles, axis=0)
            out = jnp.dot(sel[0:160, :], data, preferred_element_type=F32).astype(BF)
            for zp in range(10):
                put_tile(
                    vol,
                    0 if a == 0 else 9,
                    0 if b == 0 else 9,
                    zp,
                    out[zp * SLOTS : (zp + 1) * SLOTS],
                )


def pair_weights(wide, block):
    zero = jnp.zeros((CH, CH), BF)
    for a in range(3):
        for b in range(3):
            w0, w1, w2 = (block(a, b, c) for c in range(3))
            k = (a * 3 + b) * 2
            wide[k * 256 : k * 256 + 128, 0:128] = w0
            wide[k * 256 : k * 256 + 128, 128:256] = zero
            wide[k * 256 + 128 : k * 256 + 256, 0:128] = w1
            wide[k * 256 + 128 : k * 256 + 256, 128:256] = w0
            wide[k * 256 + 256 : k * 256 + 384, 0:128] = w2
            wide[k * 256 + 256 : k * 256 + 384, 128:256] = w1
            wide[k * 256 + 384 : k * 256 + 512, 0:128] = zero
            wide[k * 256 + 384 : k * 256 + 512, 128:256] = w2


def window(vol, x0, nx, a, b, h):
    return vol[pl.ds(x0 + a, nx), b : b + EDGE, h : h + 4].reshape(nx * EDGE * 4 * SLOTS, 256)


def conv_rows(vol, wide, x0, nx):
    taps = [window(vol, x0, nx, k // 6, k // 2 % 3, k % 2) for k in range(18)]
    return jnp.dot(jnp.concatenate(taps, axis=1), wide[...], preferred_element_type=F32)


def slot_values(coord, count, routes):
    sub = lax.broadcasted_iota(jnp.int32, (SLOTS, 128), 0)
    lane = lane_row()
    base = jnp.zeros((SLOTS, 128), jnp.int32)
    target = jnp.full((SLOTS, 128), NOWHERE, jnp.int32)
    own = jnp.full((1, 128), NOWHERE, jnp.int32)
    target_row = jnp.full((1, 128), NOWHERE, jnp.int32)
    for s in range(SLOTS):
        x, y, z = (coord[0, 0, s, d] for d in range(3))
        live = (s if s < BORDER else s - BORDER) < count[0, 0, 0 if s < BORDER else 1]
        code = position_code(x, y, z)
        place = jnp.where(live, routes[0, 0, s, 0] * CAP + routes[0, 0, s, 1], NOWHERE)
        base = jnp.where(sub == s, code, base)
        target = jnp.where(sub == s, place, target)
        own = jnp.where(lane % SLOTS == s, jnp.where(live, code, NOWHERE), own)
        target_row = jnp.where(lane % SLOTS == s, place, target_row)
    return base, target, own, target_row


def put_labels(coord, count, faces):
    lane = lane_row()
    row = jnp.zeros((1, 128), jnp.int32)
    for s in range(BORDER):
        x, y, z = (coord[0, 0, s, d] for d in range(3))
        label = jnp.where(s < count[0, 0, 0], 1 + x + TILE * y + TILE * TILE * z, 0)
        row = jnp.where(lane % BORDER == s, label, row)
    rows = jnp.broadcast_to(row.astype(F32), (LAB, 128)).astype(BF)
    for face in faces:
        face[FACE:XMSG] = rows


def occupied_lanes(count, slots, lane_slot):
    live = (lane_slot < BORDER) & (lane_slot < count[0, 0, 0])
    live = live | ((lane_slot >= BORDER) & (lane_slot - BORDER < count[0, 0, 1]))
    return jnp.where(live, 1.0, 0.0).astype(BF)


def put_faces(vol, xlo, xhi, ylo, yhi):
    r = lax.broadcasted_iota(jnp.int32, (128, 256), 0)
    k = lax.broadcasted_iota(jnp.int32, (128, 256), 1)
    chosen = one_hot(r // BORDER * SLOTS + r % BORDER, k)
    for face, at, along_y in ((xlo, 1, True), (xhi, 8, True), (ylo, 1, False), (yhi, 8, False)):
        for q in range(4):
            tiles = []
            for col in range(2):
                line = 2 * q + col + 1
                for z in range(8):
                    place = (at, line) if along_y else (line, at)
                    tiles.append(tile_at(vol, *place, z + 1))
            data = jnp.concatenate(tiles, axis=0)
            out = jnp.dot(chosen, data, preferred_element_type=F32)
            face[q * 128 : (q + 1) * 128] = out.astype(BF)


def faces_kernel(feats, mask_rows, coord, count, xlo, xhi, ylo, yhi):
    r = lax.broadcasted_iota(jnp.int32, (128, 128), 0)
    k = lax.broadcasted_iota(jnp.int32, (128, 128), 1)
    order = one_hot((r % BORDER) * 16 + r // BORDER, k)
    order = order * occupied_lanes(count, BORDER, lane_row() // 16)

    def rows(x, q, first, last):
        data = feats[:, x * 64 + q * 16 : x * 64 + (q + 1) * 16, :].reshape(128, CH)
        chosen = order[first:last] * mask_rows[x, q : q + 1, 0:128]
        return jnp.dot(chosen, data, preferred_element_type=F32).astype(BF)

    for q in range(4):
        xlo[q * 128 : (q + 1) * 128] = rows(0, q, 0, 128)
        xhi[q * 128 : (q + 1) * 128] = rows(EDGE - 1, q, 0, 128)
    for x in range(EDGE):
        ylo[x * 64 : (x + 1) * 64] = rows(x, 0, 0, 64)
        yhi[x * 64 : (x + 1) * 64] = rows(x, 3, 64, 128)
    put_labels(coord, count, (xlo, xhi, ylo, yhi))


def arrange(feats, mask_rows, count, vol, mask):
    r = lax.broadcasted_iota(jnp.int32, (256, 256), 0)
    k = lax.broadcasted_iota(jnp.int32, (256, 256), 1)
    order = one_hot((r % SLOTS) * 16 + r // SLOTS, k)
    order = order * occupied_lanes(
        count, SLOTS, lax.broadcasted_iota(jnp.int32, (1, 256), 1) // 16
    )
    ones = jnp.ones((256, CH), BF)

    def at_x(x, carry):
        for q in range(4):
            first = pl.multiple_of(x * 64 + q * 16, 16)
            data = feats[:, pl.ds(first, 16), :].reshape(256, CH)
            chosen = order * mask_rows[x, q : q + 1, :]
            out = jnp.dot(
                chosen, jnp.concatenate([data, ones], axis=1), preferred_element_type=F32
            )
            tiles = out.astype(BF).reshape(2, 8, SLOTS, 256)
            for y in range(2):
                for z in range(8):
                    put_tile(vol, x + 1, q * 2 + y + 1, z + 1, tiles[y, z, :, 0:CH])
                    mask[x, q * 2 + y, z // 2, :, (z % 2) * CH : (z % 2 + 1) * CH] = tiles[
                        y, z, :, CH : 2 * CH
                    ]
        return carry

    lax.fori_loop(0, EDGE, at_x, 0)


def forward_kernel(
    feats, mask_rows, left, right, lower, upper, coord, count, routes, weight, down, returned,
    grad_out, gxlo, gxhi, gylo, gyhi, sending, partial,
    vol, sel, wide, grad_t, route, spread, acts, subs, mask, grad_vol, sem,
):
    base, target, own, target_row = slot_values(coord, count, routes)
    pair_weights(wide, lambda a, b, c: weight[((a * 3 + b) * 3 + c) * CH :][:CH])
    arrange(feats, mask_rows, count, vol, mask)
    fill_halo(vol, sel, base, own, left, right, lower, upper)

    lane = lane_row()
    for b in range(16):
        for j in range(4):
            route[b * 16 : (b + 1) * 16, j * 128 : (j + 1) * 128] = one_hot(
                target * 16 + b, lane + 128 * j
            )
    block = lax.broadcasted_iota(jnp.int32, (16, 128), 0)
    for t in range(2 * SLOTS):
        for j in range(2):
            spread[t * 16 : (t + 1) * 16, j * 128 : (j + 1) * 128] = one_hot(
                block * 64 + t, target_row + 64 * (lane // 16 + 8 * j)
            )

    def at_hx(hx, carry):
        pre_all = conv_rows(vol, wide, 2 * hx, 2).reshape(2, 4, 2, 64, 256)
        first = pl.multiple_of(hx * 16, 16)
        grad_sub = jnp.dot(
            route[...],
            returned[:, pl.ds(first, 16), :].reshape(512, CH),
            preferred_element_type=F32,
        ).astype(BF)
        subs[pl.ds(pl.multiple_of(hx * 256, 256), 256)] = grad_sub
        grad_act = lax.dot_general(
            grad_sub, down[...], (((1,), (1,)), ((), ())), preferred_element_type=F32
        )
        total = None
        for px in range(2):
            for py in range(2):
                q = px * 2 + py
                x = 2 * hx + px
                pre = pre_all[px, :, py].reshape(256, 256)
                live = jnp.stack([mask[x, 2 * hy + py] for hy in range(4)]).reshape(256, 256)
                live = live.astype(F32)
                sig = jax.nn.sigmoid(pre)
                act = (pre * sig * live).astype(BF)
                acts[q, pl.ds(pl.multiple_of(hx * 256, 256), 256)] = act
                term = jnp.dot(
                    act, down[q * 256 : (q + 1) * 256], preferred_element_type=F32
                )
                total = term if total is None else total + term
                grad = (
                    grad_act[:, q * 256 : (q + 1) * 256]
                    * live
                    * sig
                    * (1.0 + pre * (1.0 - sig))
                )
                grad_b = grad.astype(BF)
                shaped = grad_b.reshape(4, 4, SLOTS, 256)
                turned = grad_b.T
                for hy in range(4):
                    y = 2 * hy + py
                    for p in range(4):
                        put_tile(grad_vol, x + 1, y + 1, 2 * p + 1, shaped[hy, p, :, 0:CH])
                        put_tile(grad_vol, x + 1, y + 1, 2 * p + 2, shaped[hy, p, :, CH:256])
                grad_t[hx, q] = turned
        sub = total.astype(BF)
        sent = jnp.dot(spread[...], sub, preferred_element_type=F32).astype(BF)
        sending[:, pl.ds(first, 16), :] = sent.reshape(2 * SLOTS, 16, CH)
        return carry

    lax.fori_loop(0, EDGE // 2, at_hx, 0)
    copy = pltpu.make_async_copy(grad_vol, grad_out, sem)
    copy.start()
    put_faces(grad_vol, gxlo, gxhi, gylo, gyhi)
    put_labels(coord, count, (gxlo, gxhi, gylo, gyhi))

    subs_t = subs[...].T
    for q in range(4):
        found = jnp.dot(subs_t, acts[q], preferred_element_type=F32)
        partial[3456 + q * 256 : 3456 + (q + 1) * 256] = found.T.astype(BF)

    for ab in range(9):
        a, b = ab // 3, ab % 3
        halves = []
        for h in range(2):
            total = None
            for hx in range(4):
                for q in range(4):
                    px, py = q // 2, q % 2
                    rows = jnp.stack(
                        [
                            vol[2 * hx + px + a, 2 * hy + py + b, h : h + 4]
                            for hy in range(4)
                        ]
                    ).reshape(256, 256)
                    term = jnp.dot(grad_t[hx, q], rows, preferred_element_type=F32)
                    total = term if total is None else total + term
            halves.append(total)
        low, high = halves
        taps = [
            low[0:128, 0:128] + low[128:256, 128:256],
            low[0:128, 128:256] + high[128:256, 0:128],
            high[0:128, 0:128] + high[128:256, 128:256],
        ]
        for c in range(3):
            row = (ab * 3 + c) * CH
            partial[row : row + CH] = taps[c].T.astype(BF)
    partial[4480:] = jnp.zeros((SHARD * 128 - 4480, CH), BF)
    copy.wait()


def backward_kernel(
    grad_in, mask_rows, left, right, lower, upper, coord, count, routes, weight, after,
    feat_grad, vol, sel, wide, sem,
):
    copy = pltpu.make_async_copy(grad_in, vol, sem)
    copy.start()
    base, _, own, _ = slot_values(coord, count, routes)
    pair_weights(
        wide, lambda a, b, c: weight[((2 - a) * 9 + (2 - b) * 3 + 2 - c) * CH :][:CH].T
    )
    copy.wait()
    fill_halo(vol, sel, base, own, left, right, lower, upper)
    r = lax.broadcasted_iota(jnp.int32, (256, 256), 0)
    k = lax.broadcasted_iota(jnp.int32, (256, 256), 1)
    order = one_hot(
        (r % 2) * 128 + (r // 8 % 2) * 64 + (r // 2 % 4) * 16 + r // 16, k
    )
    order = order * occupied_lanes(
        count, SLOTS, lax.broadcasted_iota(jnp.int32, (1, 256), 1) % SLOTS
    )

    def at_hx(hx, carry):
        back = conv_rows(vol, wide, 2 * hx, 2).astype(BF).reshape(2, 4, 128, 256)
        for px in range(2):
            for q in range(4):
                x = 2 * hx + px
                data = jnp.concatenate(
                    [back[px, q, :, 0:CH], back[px, q, :, CH:256]], axis=0
                )
                chosen = order * mask_rows[x, q : q + 1, :]
                out = jnp.dot(chosen, data, preferred_element_type=F32).astype(BF)
                first = pl.multiple_of(x * 64 + q * 16, 16)
                feat_grad[:, pl.ds(first, 16), :] = out.reshape(SLOTS, 16, CH)
        return carry

    lax.fori_loop(0, EDGE // 2, at_hx, 0)


VMEM_LIMIT = 56 * 1024 * 1024
VOLUME = (10, 10, 5, SLOTS, 256)


def whole(count):
    return [pl.BlockSpec(memory_space=pltpu.VMEM)] * count


def scalar(count):
    return [pl.BlockSpec(memory_space=pltpu.SMEM)] * count


def microseconds(time):
    return pl.CostEstimate(flops=int(time * 1.1e9), bytes_accessed=1 << 20, transcendentals=0)


def shift(value, axis, step):
    count = lax.axis_size(axis)
    if step > 0:
        pairs = [(i, i + 1) for i in range(count - 1)]
    else:
        pairs = [(i + 1, i) for i in range(count - 1)]
    return lax.ppermute(value, axis, pairs)


def exchange(xlo, xhi, ylo, yhi):
    left = shift(xhi, "gx", 1)
    right = shift(xlo, "gx", -1)
    ends = [left[FACE:XMSG], right[FACE:XMSG]]
    up = jnp.concatenate([yhi, left[FACE - 64 : FACE], right[FACE - 64 : FACE]] + ends)
    down = jnp.concatenate([ylo, left[0:64], right[0:64]] + ends)
    lower = shift(up, "gy", 1)
    upper = shift(down, "gy", -1)
    return left, right, lower, upper


def per_device(
    feats, voxel_mask, brick_coord, brick_count, route, conv_weight, down_weight, coarse_grad
):
    tiles_x = lax.axis_size("gx")
    tiles_y = lax.axis_size("gy")
    devices = tiles_x * tiles_y
    active = voxel_mask[0, 0].astype(BF)
    mask_rows = active.reshape(SLOTS, EDGE, 4, 16).transpose(1, 2, 0, 3).reshape(EDGE, 4, 256)
    by_pair = active.reshape(SLOTS, EDGE, 4, 2, 4, 2)
    back_rows = by_pair.transpose(1, 2, 5, 3, 4, 0).reshape(EDGE, 4, 256)
    scalars = (brick_coord, brick_count, route)

    face = jax.ShapeDtypeStruct((XMSG, CH), BF)
    volume = jax.ShapeDtypeStruct(VOLUME, BF)
    faces = pl.pallas_call(
        faces_kernel,
        grid=(1,),
        out_shape=(face,) * 4,
        in_specs=[pl.BlockSpec((BORDER, VOX, CH), lambda i: (0, 0, 0))] + whole(1) + scalar(2),
        out_specs=tuple(whole(4)),
        compiler_params=pltpu.CompilerParams(vmem_limit_bytes=VMEM_LIMIT),
        cost_estimate=microseconds(2),
        name="faces",
    )(feats[0, 0], mask_rows, *scalars[:2])
    around = exchange(*faces)
    returned = lax.all_to_all(
        coarse_grad[0, 0].reshape(tiles_x, CAP * 64, CH), "gx", 0, 0, tiled=True
    ).reshape(2 * SLOTS, 64, CH)

    grad_vol, gxlo, gxhi, gylo, gyhi, sending, partial = pl.pallas_call(
        forward_kernel,
        out_shape=(volume,)
        + (face,) * 4
        + (
            jax.ShapeDtypeStruct((2 * SLOTS, 64, CH), BF),
            jax.ShapeDtypeStruct((SHARD * 128, CH), BF),
        ),
        in_specs=whole(6) + scalar(3) + whole(3),
        out_specs=(pl.BlockSpec(memory_space=pl.ANY),) + tuple(whole(6)),
        scratch_shapes=[
            pltpu.VMEM(VOLUME, BF),
            pltpu.VMEM((320, 384), BF),
            pltpu.VMEM((18 * 256, 256), BF),
            pltpu.VMEM((4, 4, 256, 256), BF),
            pltpu.VMEM((256, 512), BF),
            pltpu.VMEM((512, 256), BF),
            pltpu.VMEM((4, 1024, 256), BF),
            pltpu.VMEM((1024, CH), BF),
            pltpu.VMEM((8, 8, 4, SLOTS, 256), BF),
            pltpu.VMEM(VOLUME, BF),
            pltpu.SemaphoreType.DMA(()),
        ],
        compiler_params=pltpu.CompilerParams(vmem_limit_bytes=VMEM_LIMIT),
        cost_estimate=microseconds(34),
        name="forward",
    )(feats[0, 0], mask_rows, *around, *scalars, conv_weight, down_weight, returned)

    around = exchange(gxlo, gxhi, gylo, gyhi)
    parts = lax.all_to_all(
        partial.reshape(devices, SHARD, CH), ("gx", "gy"), 0, 0, tiled=True
    )
    feat_grad = pl.pallas_call(
        backward_kernel,
        out_shape=jax.ShapeDtypeStruct((SLOTS, VOX, CH), BF),
        in_specs=[pl.BlockSpec(memory_space=pl.ANY)]
        + whole(5)
        + scalar(3)
        + whole(1)
        + [pl.BlockSpec(memory_space=pl.ANY)],
        out_specs=whole(1)[0],
        scratch_shapes=[
            pltpu.VMEM(VOLUME, BF),
            pltpu.VMEM((320, 384), BF),
            pltpu.VMEM((18 * 256, 256), BF),
            pltpu.SemaphoreType.DMA(()),
        ],
        compiler_params=pltpu.CompilerParams(vmem_limit_bytes=VMEM_LIMIT),
        cost_estimate=microseconds(18),
        name="backward",
    )(grad_vol, back_rows, *around, *scalars, conv_weight, partial)

    total = jnp.sum(parts.astype(F32), axis=0).astype(BF)
    coarse = lax.all_to_all(
        sending.reshape(tiles_x, CAP * 64, CH), "gx", 0, 0, tiled=True
    ).reshape(1, 1, 2 * SLOTS, 64, CH)
    sums = lax.all_to_all(
        jnp.broadcast_to(total[None], (devices, SHARD, CH)), ("gx", "gy"), 0, 0, tiled=True
    ).reshape(devices * SHARD, CH)
    total_slots = devices * SLOTS
    conv_grad = sums[:3456].astype(F32) * (1.0 / math.sqrt(total_slots * VOX))
    down_grad = sums[3456:4480].astype(F32) * (1.0 / math.sqrt(total_slots * VOX // 8))
    return (coarse, feat_grad[None, None], conv_grad, down_grad)


def solution(mesh):
    in_specs = (
        P("gx", "gy", None, None, None),
        P("gx", "gy", None, None),
        P("gx", "gy", None, None),
        P("gx", "gy", None),
        P("gx", "gy", None, None),
        P(),
        P(),
        P("gx", "gy", None, None, None),
    )
    out_specs = (P("gx", "gy", None, None, None), P("gx", "gy", None, None, None), P(), P())
    return jax.shard_map(
        per_device, mesh=mesh, in_specs=in_specs, out_specs=out_specs, check_vma=False
    )
```

```python
import math

import jax
import jax.numpy as jnp
import numpy as np
from jax import lax
from jax.experimental import pallas as pl
from jax.experimental.pallas import tpu as pltpu
from jax.sharding import PartitionSpec as P

CH = 128
EDGE = 8
VOX = 512
TILE = 4
SLOTS = 16
BORDER = 8
CAP = 2
BF = jnp.bfloat16
F32 = jnp.float32
FACE = 64 * BORDER
LAB = 16
XMSG = FACE + LAB
YMSG = XMSG + 2 * 64 + 2 * LAB
SHARD = 40
VSTEP = 4096
NOWHERE = -(1 << 20)


def position_code(x, y, z):
    return (x + TILE) * 96 + (y + TILE) * 8 + z + 1


def label_code(row, shift_x, shift_y):
    packed = row.astype(F32).astype(jnp.int32) - 1
    code = position_code(
        (packed & 3) + shift_x * TILE, ((packed >> 2) & 3) + shift_y * TILE, packed >> 4
    )
    return jnp.where(packed < 0, NOWHERE, code)


def one_hot(left, right):
    return jnp.where(left == right, 1.0, 0.0).astype(BF)


def tap_delta(a, b, c):
    return (a - 1) * 96 + (b - 1) * 8 + (c - 1)


def lane_row():
    return lax.broadcasted_iota(jnp.int32, (1, 128), 1)


def tile_at(vol, xp, yp, zp):
    return vol[xp, yp, zp // 2, :, (zp % 2) * CH : (zp % 2 + 1) * CH]


def put_tile(vol, xp, yp, zp, value):
    vol[xp, yp, zp // 2, :, (zp % 2) * CH : (zp % 2 + 1) * CH] = value


def fill_halo(vol, sel, base, own, left, right, lower, upper):
    lane = lane_row()
    own = own + VSTEP * (lane // SLOTS)
    nothing = jnp.zeros((SLOTS, 128), BF)
    zs = [7, 0, 1, 2, 3, 4, 5, 6, 7, 0]
    cs = [0] + [1] * 8 + [2]

    sides = [
        (0, 1, left, -1, 0),
        (2, 1, right, 1, 0),
        (1, 0, lower, 0, -1),
        (1, 2, upper, 0, 1),
    ]
    for a, b, msg, sx, sy in sides:
        far = label_code(msg[FACE : FACE + 1], sx, sy) + VSTEP * (lane // BORDER)
        for zp in range(10):
            for col in range(2):
                rows = pl.ds((zp * 2 + col) * SLOTS, SLOTS)
                want = base + (tap_delta(a, b, cs[zp]) + VSTEP * (col * 8 + zs[zp]))
                here = one_hot(want, own + VSTEP * 8 * col)
                sel[rows, col * 128 : (col + 1) * 128] = here
                sel[rows, (1 - col) * 128 : (2 - col) * 128] = nothing
                sel[rows, 256:384] = one_hot(want, far)
        for half in range(2):
            parts = []
            for k in range(2):
                first = (half * 2 + k) * 2
                tiles = []
                for col in range(2):
                    for z in range(8):
                        if b == 1:
                            tiles.append(tile_at(vol, 8 if a == 0 else 1, first + col + 1, z + 1))
                        else:
                            tiles.append(tile_at(vol, first + col + 1, 8 if b == 0 else 1, z + 1))
                tiles.append(msg[first * 64 : (first + 2) * 64])
                parts.append(jnp.concatenate(tiles, axis=0))
            data = jnp.concatenate(parts, axis=1)
            out = jnp.dot(sel[0:320, :], data, preferred_element_type=F32).astype(BF)
            for k in range(2):
                for zp in range(10):
                    for col in range(2):
                        at = (half * 2 + k) * 2 + col + 1
                        row = (zp * 2 + col) * SLOTS
                        value = out[row : row + SLOTS, k * 128 : (k + 1) * 128]
                        if b == 1:
                            put_tile(vol, 0 if a == 0 else 9, at, zp, value)
                        else:
                            put_tile(vol, at, 0 if b == 0 else 9, zp, value)

    for c in (0, 2):
        for v in range(16):
            rows = pl.ds(v * SLOTS, SLOTS)
            j = v // 8
            want = base + (tap_delta(1, 1, c) + VSTEP * v)
            sel[rows, j * 128 : (j + 1) * 128] = one_hot(want, own + VSTEP * 8 * j)
            sel[rows, (1 - j) * 128 : (2 - j) * 128] = nothing
        for half in range(2):
            parts = []
            for k in range(2):
                tiles = []
                for v in range(16):
                    at = (half * 2 + k) * 16 + v
                    tiles.append(tile_at(vol, at // 8 + 1, at % 8 + 1, 8 if c == 0 else 1))
                parts.append(jnp.concatenate(tiles, axis=0))
            data = jnp.concatenate(parts, axis=1)
            out = jnp.dot(sel[0:256, 0:256], data, preferred_element_type=F32).astype(BF)
            for k in range(2):
                for v in range(16):
                    at = (half * 2 + k) * 16 + v
                    put_tile(
                        vol,
                        at // 8 + 1,
                        at % 8 + 1,
                        0 if c == 0 else 9,
                        out[v * SLOTS : (v + 1) * SLOTS, k * 128 : (k + 1) * 128],
                    )

    for a in (0, 2):
        for b in (0, 2):
            side = left if a == 0 else right
            face = lower if b == 0 else upper
            side_code = label_code(side[FACE : FACE + 1], a - 1, 0)
            face_code = label_code(face[FACE : FACE + 1], 0, b - 1)
            corner_at = XMSG if a == 0 else XMSG + 64
            corner_lab = XMSG + 128 if a == 0 else XMSG + 128 + LAB
            corner_code = label_code(face[corner_lab : corner_lab + 1], a - 1, b - 1)
            voxel = VSTEP * (lane % 64 // BORDER)
            beside = jnp.where(lane < 64, side_code, face_code) + voxel
            across = jnp.where(lane < 64, corner_code, NOWHERE) + voxel
            for zp in range(10):
                rows = pl.ds(zp * SLOTS, SLOTS)
                want = base + (tap_delta(a, b, cs[zp]) + VSTEP * zs[zp])
                sel[rows, 0:128] = one_hot(want, own)
                sel[rows, 128:256] = one_hot(want, beside)
                sel[rows, 256:384] = one_hot(want, across)
            xs = 8 if a == 0 else 1
            ys = 8 if b == 0 else 1
            tiles = [tile_at(vol, xs, ys, z + 1) for z in range(8)]
            line_y = (7 if b == 0 else 0) * 64
            line_x = (7 if a == 0 else 0) * 64
            tiles.append(side[line_y : line_y + 64])
            tiles.append(face[line_x : line_x + 64])
            tiles.append(face[corner_at : corner_at + 64])
            tiles.append(jnp.zeros((64, CH), BF))
            data = jnp.concatenate(tiles, axis=0)
            out = jnp.dot(sel[0:160, :], data, preferred_element_type=F32).astype(BF)
            for zp in range(10):
                put_tile(
                    vol,
                    0 if a == 0 else 9,
                    0 if b == 0 else 9,
                    zp,
                    out[zp * SLOTS : (zp + 1) * SLOTS],
                )


def pair_weights(wide, block):
    zero = jnp.zeros((CH, CH), BF)
    for a in range(3):
        for b in range(3):
            w0, w1, w2 = (block(a, b, c) for c in range(3))
            k = (a * 3 + b) * 2
            wide[k * 256 : k * 256 + 128, 0:128] = w0
            wide[k * 256 : k * 256 + 128, 128:256] = zero
            wide[k * 256 + 128 : k * 256 + 256, 0:128] = w1
            wide[k * 256 + 128 : k * 256 + 256, 128:256] = w0
            wide[k * 256 + 256 : k * 256 + 384, 0:128] = w2
            wide[k * 256 + 256 : k * 256 + 384, 128:256] = w1
            wide[k * 256 + 384 : k * 256 + 512, 0:128] = zero
            wide[k * 256 + 384 : k * 256 + 512, 128:256] = w2


def window(vol, x0, nx, a, b, h):
    return vol[pl.ds(x0 + a, nx), b : b + EDGE, h : h + 4].reshape(nx * EDGE * 4 * SLOTS, 256)


def conv_rows(vol, wide, x0, nx):
    taps = [window(vol, x0, nx, k // 6, k // 2 % 3, k % 2) for k in range(18)]
    return jnp.dot(jnp.concatenate(taps, axis=1), wide[...], preferred_element_type=F32)


def slot_values(coord, count, routes):
    sub = lax.broadcasted_iota(jnp.int32, (SLOTS, 128), 0)
    lane = lane_row()
    base = jnp.zeros((SLOTS, 128), jnp.int32)
    target = jnp.full((SLOTS, 128), NOWHERE, jnp.int32)
    own = jnp.full((1, 128), NOWHERE, jnp.int32)
    target_row = jnp.full((1, 128), NOWHERE, jnp.int32)
    for s in range(SLOTS):
        x, y, z = (coord[0, 0, s, d] for d in range(3))
        live = (s if s < BORDER else s - BORDER) < count[0, 0, 0 if s < BORDER else 1]
        code = position_code(x, y, z)
        place = jnp.where(live, routes[0, 0, s, 0] * CAP + routes[0, 0, s, 1], NOWHERE)
        base = jnp.where(sub == s, code, base)
        target = jnp.where(sub == s, place, target)
        own = jnp.where(lane % SLOTS == s, jnp.where(live, code, NOWHERE), own)
        target_row = jnp.where(lane % SLOTS == s, place, target_row)
    return base, target, own, target_row


def put_labels(coord, count, faces):
    lane = lane_row()
    row = jnp.zeros((1, 128), jnp.int32)
    for s in range(BORDER):
        x, y, z = (coord[0, 0, s, d] for d in range(3))
        label = jnp.where(s < count[0, 0, 0], 1 + x + TILE * y + TILE * TILE * z, 0)
        row = jnp.where(lane % BORDER == s, label, row)
    rows = jnp.broadcast_to(row.astype(F32), (LAB, 128)).astype(BF)
    for face in faces:
        face[FACE:XMSG] = rows


def occupied_lanes(count, slots, lane_slot):
    live = (lane_slot < BORDER) & (lane_slot < count[0, 0, 0])
    live = live | ((lane_slot >= BORDER) & (lane_slot - BORDER < count[0, 0, 1]))
    return jnp.where(live, 1.0, 0.0).astype(BF)


def put_faces(vol, xlo, xhi, ylo, yhi):
    r = lax.broadcasted_iota(jnp.int32, (128, 256), 0)
    k = lax.broadcasted_iota(jnp.int32, (128, 256), 1)
    chosen = one_hot(r // BORDER * SLOTS + r % BORDER, k)
    for face, at, along_y in ((xlo, 1, True), (xhi, 8, True), (ylo, 1, False), (yhi, 8, False)):
        for q in range(4):
            tiles = []
            for col in range(2):
                line = 2 * q + col + 1
                for z in range(8):
                    place = (at, line) if along_y else (line, at)
                    tiles.append(tile_at(vol, *place, z + 1))
            data = jnp.concatenate(tiles, axis=0)
            out = jnp.dot(chosen, data, preferred_element_type=F32)
            face[q * 128 : (q + 1) * 128] = out.astype(BF)


def faces_kernel(feats, mask_rows, coord, count, xlo, xhi, ylo, yhi):
    r = lax.broadcasted_iota(jnp.int32, (128, 128), 0)
    k = lax.broadcasted_iota(jnp.int32, (128, 128), 1)
    order = one_hot((r % BORDER) * 16 + r // BORDER, k)
    order = order * occupied_lanes(count, BORDER, lane_row() // 16)

    def rows(x, q, first, last):
        data = feats[:, x * 64 + q * 16 : x * 64 + (q + 1) * 16, :].reshape(128, CH)
        chosen = order[first:last] * mask_rows[x, q : q + 1, 0:128]
        return jnp.dot(chosen, data, preferred_element_type=F32).astype(BF)

    for q in range(4):
        xlo[q * 128 : (q + 1) * 128] = rows(0, q, 0, 128)
        xhi[q * 128 : (q + 1) * 128] = rows(EDGE - 1, q, 0, 128)
    for x in range(EDGE):
        ylo[x * 64 : (x + 1) * 64] = rows(x, 0, 0, 64)
        yhi[x * 64 : (x + 1) * 64] = rows(x, 3, 64, 128)
    put_labels(coord, count, (xlo, xhi, ylo, yhi))


def arrange(feats, mask_rows, count, vol, mask):
    r = lax.broadcasted_iota(jnp.int32, (256, 256), 0)
    k = lax.broadcasted_iota(jnp.int32, (256, 256), 1)
    order = one_hot((r % SLOTS) * 16 + r // SLOTS, k)
    order = order * occupied_lanes(
        count, SLOTS, lax.broadcasted_iota(jnp.int32, (1, 256), 1) // 16
    )
    ones = jnp.ones((256, CH), BF)

    def at_x(x, carry):
        for q in range(4):
            first = pl.multiple_of(x * 64 + q * 16, 16)
            data = feats[:, pl.ds(first, 16), :].reshape(256, CH)
            chosen = order * mask_rows[x, q : q + 1, :]
            out = jnp.dot(
                chosen, jnp.concatenate([data, ones], axis=1), preferred_element_type=F32
            )
            tiles = out.astype(BF).reshape(2, 8, SLOTS, 256)
            for y in range(2):
                for z in range(8):
                    put_tile(vol, x + 1, q * 2 + y + 1, z + 1, tiles[y, z, :, 0:CH])
                    mask[x, q * 2 + y, z // 2, :, (z % 2) * CH : (z % 2 + 1) * CH] = tiles[
                        y, z, :, CH : 2 * CH
                    ]
        return carry

    lax.fori_loop(0, EDGE, at_x, 0)


def forward_kernel(
    feats, mask_rows, left, right, lower, upper, coord, count, routes, weight, down, returned,
    grad_out, gxlo, gxhi, gylo, gyhi, sending, partial,
    vol, sel, wide, grad_t, route, spread, acts, subs, mask, grad_vol, sem,
):
    base, target, own, target_row = slot_values(coord, count, routes)
    pair_weights(wide, lambda a, b, c: weight[((a * 3 + b) * 3 + c) * CH :][:CH])
    arrange(feats, mask_rows, count, vol, mask)
    fill_halo(vol, sel, base, own, left, right, lower, upper)

    lane = lane_row()
    for b in range(16):
        for j in range(4):
            route[b * 16 : (b + 1) * 16, j * 128 : (j + 1) * 128] = one_hot(
                target * 16 + b, lane + 128 * j
            )
    block = lax.broadcasted_iota(jnp.int32, (16, 128), 0)
    for t in range(2 * SLOTS):
        for j in range(2):
            spread[t * 16 : (t + 1) * 16, j * 128 : (j + 1) * 128] = one_hot(
                block * 64 + t, target_row + 64 * (lane // 16 + 8 * j)
            )

    def at_hx(hx, carry):
        pre_all = conv_rows(vol, wide, 2 * hx, 2).reshape(2, 4, 2, 64, 256)
        first = pl.multiple_of(hx * 16, 16)
        grad_sub = jnp.dot(
            route[...],
            returned[:, pl.ds(first, 16), :].reshape(512, CH),
            preferred_element_type=F32,
        ).astype(BF)
        subs[pl.ds(pl.multiple_of(hx * 256, 256), 256)] = grad_sub
        grad_act = lax.dot_general(
            grad_sub, down[...], (((1,), (1,)), ((), ())), preferred_element_type=F32
        )
        total = None
        for px in range(2):
            for py in range(2):
                q = px * 2 + py
                x = 2 * hx + px
                pre = pre_all[px, :, py].reshape(256, 256)
                live = jnp.stack([mask[x, 2 * hy + py] for hy in range(4)]).reshape(256, 256)
                live = live.astype(F32)
                sig = jax.nn.sigmoid(pre)
                act = (pre * sig * live).astype(BF)
                acts[q, pl.ds(pl.multiple_of(hx * 256, 256), 256)] = act
                term = jnp.dot(
                    act, down[q * 256 : (q + 1) * 256], preferred_element_type=F32
                )
                total = term if total is None else total + term
                grad = (
                    grad_act[:, q * 256 : (q + 1) * 256]
                    * live
                    * sig
                    * (1.0 + pre * (1.0 - sig))
                )
                grad_b = grad.astype(BF)
                shaped = grad_b.reshape(4, 4, SLOTS, 256)
                turned = grad_b.T
                for hy in range(4):
                    y = 2 * hy + py
                    for p in range(4):
                        put_tile(grad_vol, x + 1, y + 1, 2 * p + 1, shaped[hy, p, :, 0:CH])
                        put_tile(grad_vol, x + 1, y + 1, 2 * p + 2, shaped[hy, p, :, CH:256])
                grad_t[hx, q] = turned
        sub = total.astype(BF)
        sent = jnp.dot(spread[...], sub, preferred_element_type=F32).astype(BF)
        sending[:, pl.ds(first, 16), :] = sent.reshape(2 * SLOTS, 16, CH)
        return carry

    lax.fori_loop(0, EDGE // 2, at_hx, 0)
    copy = pltpu.make_async_copy(grad_vol, grad_out, sem)
    copy.start()
    put_faces(grad_vol, gxlo, gxhi, gylo, gyhi)
    put_labels(coord, count, (gxlo, gxhi, gylo, gyhi))

    subs_t = subs[...].T
    for q in range(4):
        found = jnp.dot(subs_t, acts[q], preferred_element_type=F32)
        partial[3456 + q * 256 : 3456 + (q + 1) * 256] = found.T.astype(BF)

    for ab in range(9):
        a, b = ab // 3, ab % 3
        halves = []
        for h in range(2):
            total = None
            for hx in range(4):
                for q in range(4):
                    px, py = q // 2, q % 2
                    rows = jnp.stack(
                        [
                            vol[2 * hx + px + a, 2 * hy + py + b, h : h + 4]
                            for hy in range(4)
                        ]
                    ).reshape(256, 256)
                    term = jnp.dot(grad_t[hx, q], rows, preferred_element_type=F32)
                    total = term if total is None else total + term
            halves.append(total)
        low, high = halves
        taps = [
            low[0:128, 0:128] + low[128:256, 128:256],
            low[0:128, 128:256] + high[128:256, 0:128],
            high[0:128, 0:128] + high[128:256, 128:256],
        ]
        for c in range(3):
            row = (ab * 3 + c) * CH
            partial[row : row + CH] = taps[c].T.astype(BF)
    partial[4480:] = jnp.zeros((SHARD * 128 - 4480, CH), BF)
    copy.wait()


def backward_kernel(
    grad_in, mask_rows, left, right, lower, upper, coord, count, routes, weight,
    feat_grad, vol, sel, wide, sem,
):
    copy = pltpu.make_async_copy(grad_in, vol, sem)
    copy.start()
    base, _, own, _ = slot_values(coord, count, routes)
    pair_weights(
        wide, lambda a, b, c: weight[((2 - a) * 9 + (2 - b) * 3 + 2 - c) * CH :][:CH].T
    )
    copy.wait()
    fill_halo(vol, sel, base, own, left, right, lower, upper)
    r = lax.broadcasted_iota(jnp.int32, (256, 256), 0)
    k = lax.broadcasted_iota(jnp.int32, (256, 256), 1)
    order = one_hot(
        (r % 2) * 128 + (r // 8 % 2) * 64 + (r // 2 % 4) * 16 + r // 16, k
    )
    order = order * occupied_lanes(
        count, SLOTS, lax.broadcasted_iota(jnp.int32, (1, 256), 1) % SLOTS
    )

    def at_hx(hx, carry):
        back = conv_rows(vol, wide, 2 * hx, 2).astype(BF).reshape(2, 4, 128, 256)
        for px in range(2):
            for q in range(4):
                x = 2 * hx + px
                data = jnp.concatenate(
                    [back[px, q, :, 0:CH], back[px, q, :, CH:256]], axis=0
                )
                chosen = order * mask_rows[x, q : q + 1, :]
                out = jnp.dot(chosen, data, preferred_element_type=F32).astype(BF)
                first = pl.multiple_of(x * 64 + q * 16, 16)
                feat_grad[:, pl.ds(first, 16), :] = out.reshape(SLOTS, 16, CH)
        return carry

    lax.fori_loop(0, EDGE // 2, at_hx, 0)


def later_kernel(value, after, same):
    same[...] = value[...]


VMEM_LIMIT = 56 * 1024 * 1024
VOLUME = (10, 10, 5, SLOTS, 256)


def whole(count):
    return [pl.BlockSpec(memory_space=pltpu.VMEM)] * count


def scalar(count):
    return [pl.BlockSpec(memory_space=pltpu.SMEM)] * count


def microseconds(time):
    return pl.CostEstimate(flops=int(time * 1.1e9), bytes_accessed=1 << 20, transcendentals=0)


def shift(value, axis, step):
    count = lax.axis_size(axis)
    if step > 0:
        pairs = [(i, i + 1) for i in range(count - 1)]
    else:
        pairs = [(i + 1, i) for i in range(count - 1)]
    return lax.ppermute(value, axis, pairs)


def exchange(xlo, xhi, ylo, yhi):
    left = shift(xhi, "gx", 1)
    right = shift(xlo, "gx", -1)
    ends = [left[FACE:XMSG], right[FACE:XMSG]]
    up = jnp.concatenate([yhi, left[FACE - 64 : FACE], right[FACE - 64 : FACE]] + ends)
    down = jnp.concatenate([ylo, left[0:64], right[0:64]] + ends)
    lower = shift(up, "gy", 1)
    upper = shift(down, "gy", -1)
    return left, right, lower, upper


def per_device(
    feats, voxel_mask, brick_coord, brick_count, route, conv_weight, down_weight, coarse_grad
):
    tiles_x = lax.axis_size("gx")
    tiles_y = lax.axis_size("gy")
    devices = tiles_x * tiles_y
    active = voxel_mask[0, 0].astype(BF)
    mask_rows = active.reshape(SLOTS, EDGE, 4, 16).transpose(1, 2, 0, 3).reshape(EDGE, 4, 256)
    by_pair = active.reshape(SLOTS, EDGE, 4, 2, 4, 2)
    back_rows = by_pair.transpose(1, 2, 5, 3, 4, 0).reshape(EDGE, 4, 256)
    scalars = (brick_coord, brick_count, route)

    face = jax.ShapeDtypeStruct((XMSG, CH), BF)
    volume = jax.ShapeDtypeStruct(VOLUME, BF)
    faces = pl.pallas_call(
        faces_kernel,
        grid=(1,),
        out_shape=(face,) * 4,
        in_specs=[pl.BlockSpec((BORDER, VOX, CH), lambda i: (0, 0, 0))] + whole(1) + scalar(2),
        out_specs=tuple(whole(4)),
        compiler_params=pltpu.CompilerParams(vmem_limit_bytes=VMEM_LIMIT),
        cost_estimate=microseconds(2),
        name="faces",
    )(feats[0, 0], mask_rows, *scalars[:2])
    around = exchange(*faces)
    cotangents = pl.pallas_call(
        later_kernel,
        out_shape=jax.ShapeDtypeStruct((tiles_x, CAP * 64, CH), BF),
        in_specs=whole(1) + [pl.BlockSpec(memory_space=pl.ANY)],
        out_specs=whole(1)[0],
        compiler_params=pltpu.CompilerParams(vmem_limit_bytes=VMEM_LIMIT),
        cost_estimate=microseconds(1),
        name="later",
    )(coarse_grad[0, 0].reshape(tiles_x, CAP * 64, CH), around[0])
    returned = lax.all_to_all(
        cotangents, "gx", 0, 0, tiled=True
    ).reshape(2 * SLOTS, 64, CH)

    grad_vol, gxlo, gxhi, gylo, gyhi, sending, partial = pl.pallas_call(
        forward_kernel,
        out_shape=(volume,)
        + (face,) * 4
        + (
            jax.ShapeDtypeStruct((2 * SLOTS, 64, CH), BF),
            jax.ShapeDtypeStruct((SHARD * 128, CH), BF),
        ),
        in_specs=whole(6) + scalar(3) + whole(3),
        out_specs=(pl.BlockSpec(memory_space=pl.ANY),) + tuple(whole(6)),
        scratch_shapes=[
            pltpu.VMEM(VOLUME, BF),
            pltpu.VMEM((320, 384), BF),
            pltpu.VMEM((18 * 256, 256), BF),
            pltpu.VMEM((4, 4, 256, 256), BF),
            pltpu.VMEM((256, 512), BF),
            pltpu.VMEM((512, 256), BF),
            pltpu.VMEM((4, 1024, 256), BF),
            pltpu.VMEM((1024, CH), BF),
            pltpu.VMEM((8, 8, 4, SLOTS, 256), BF),
            pltpu.VMEM(VOLUME, BF),
            pltpu.SemaphoreType.DMA(()),
        ],
        compiler_params=pltpu.CompilerParams(vmem_limit_bytes=VMEM_LIMIT),
        cost_estimate=microseconds(34),
        name="forward",
    )(feats[0, 0], mask_rows, *around, *scalars, conv_weight, down_weight, returned)

    around = exchange(gxlo, gxhi, gylo, gyhi)
    shares = tiles_x * SHARD
    parts = lax.all_to_all(partial.reshape(tiles_y, shares, CH), "gy", 0, 0, tiled=True)
    feat_grad = pl.pallas_call(
        backward_kernel,
        out_shape=jax.ShapeDtypeStruct((SLOTS, VOX, CH), BF),
        in_specs=[pl.BlockSpec(memory_space=pl.ANY)]
        + whole(5)
        + scalar(3)
        + whole(1),
        out_specs=whole(1)[0],
        scratch_shapes=[
            pltpu.VMEM(VOLUME, BF),
            pltpu.VMEM((320, 384), BF),
            pltpu.VMEM((18 * 256, 256), BF),
            pltpu.SemaphoreType.DMA(()),
        ],
        compiler_params=pltpu.CompilerParams(vmem_limit_bytes=VMEM_LIMIT),
        cost_estimate=microseconds(18),
        name="backward",
    )(grad_vol, back_rows, *around, *scalars, conv_weight)

    total = jnp.sum(parts.astype(F32), axis=0).astype(BF).reshape(tiles_x, SHARD, CH)
    message = jnp.concatenate([sending.reshape(tiles_x, CAP * 64, CH), total], axis=1)
    parts = lax.all_to_all(message, "gx", 0, 0, tiled=True)
    coarse = parts[:, : CAP * 64].reshape(1, 1, 2 * SLOTS, 64, CH)
    total = jnp.sum(parts[:, CAP * 64 :].astype(F32), axis=0).astype(BF)
    sums = lax.all_to_all(
        jnp.broadcast_to(total[None], (devices, SHARD, CH)), ("gy", "gx"), 0, 0, tiled=True
    ).reshape(devices * SHARD, CH)
    total_slots = devices * SLOTS
    conv_grad = sums[:3456].astype(F32) * (1.0 / math.sqrt(total_slots * VOX))
    down_grad = sums[3456:4480].astype(F32) * (1.0 / math.sqrt(total_slots * VOX // 8))
    return (coarse, feat_grad[None, None], conv_grad, down_grad)


def solution(mesh):
    in_specs = (
        P("gx", "gy", None, None, None),
        P("gx", "gy", None, None),
        P("gx", "gy", None, None),
        P("gx", "gy", None),
        P("gx", "gy", None, None),
        P(),
        P(),
        P("gx", "gy", None, None, None),
    )
    out_specs = (P("gx", "gy", None, None, None), P("gx", "gy", None, None, None), P(), P())
    return jax.shard_map(
        per_device, mesh=mesh, in_specs=in_specs, out_specs=out_specs, check_vma=False
    )
```

```python
import math

import jax
import jax.numpy as jnp
import numpy as np
from jax import lax
from jax.experimental import pallas as pl
from jax.experimental.pallas import tpu as pltpu
from jax.sharding import PartitionSpec as P

CH = 128
EDGE = 8
VOX = 512
TILE = 4
SLOTS = 16
BORDER = 8
CAP = 2
BF = jnp.bfloat16
F32 = jnp.float32
FACE = 64 * BORDER
LAB = 16
XMSG = FACE + LAB
YMSG = XMSG + 2 * 64 + 2 * LAB
SHARD = 40
VSTEP = 4096
NOWHERE = -(1 << 20)


def position_code(x, y, z):
    return (x + TILE) * 96 + (y + TILE) * 8 + z + 1


def label_code(row, shift_x, shift_y):
    packed = row.astype(F32).astype(jnp.int32) - 1
    code = position_code(
        (packed & 3) + shift_x * TILE, ((packed >> 2) & 3) + shift_y * TILE, packed >> 4
    )
    return jnp.where(packed < 0, NOWHERE, code)


def one_hot(left, right):
    return jnp.where(left == right, 1.0, 0.0).astype(BF)


def tap_delta(a, b, c):
    return (a - 1) * 96 + (b - 1) * 8 + (c - 1)


def lane_row():
    return lax.broadcasted_iota(jnp.int32, (1, 128), 1)


def tile_at(vol, xp, yp, zp):
    return vol[xp, yp, zp // 2, :, (zp % 2) * CH : (zp % 2 + 1) * CH]


def put_tile(vol, xp, yp, zp, value):
    vol[xp, yp, zp // 2, :, (zp % 2) * CH : (zp % 2 + 1) * CH] = value


def fill_halo(vol, sel, base, own, left, right, lower, upper):
    lane = lane_row()
    own = own + VSTEP * (lane // SLOTS)
    nothing = jnp.zeros((SLOTS, 128), BF)
    zs = [7, 0, 1, 2, 3, 4, 5, 6, 7, 0]
    cs = [0] + [1] * 8 + [2]

    sides = [
        (0, 1, left, -1, 0),
        (2, 1, right, 1, 0),
        (1, 0, lower, 0, -1),
        (1, 2, upper, 0, 1),
    ]
    for a, b, msg, sx, sy in sides:
        far = label_code(msg[FACE : FACE + 1], sx, sy) + VSTEP * (lane // BORDER)
        for zp in range(10):
            for col in range(2):
                rows = pl.ds((zp * 2 + col) * SLOTS, SLOTS)
                want = base + (tap_delta(a, b, cs[zp]) + VSTEP * (col * 8 + zs[zp]))
                here = one_hot(want, own + VSTEP * 8 * col)
                sel[rows, col * 128 : (col + 1) * 128] = here
                sel[rows, (1 - col) * 128 : (2 - col) * 128] = nothing
                sel[rows, 256:384] = one_hot(want, far)
        for half in range(2):
            parts = []
            for k in range(2):
                first = (half * 2 + k) * 2
                tiles = []
                for col in range(2):
                    for z in range(8):
                        if b == 1:
                            tiles.append(tile_at(vol, 8 if a == 0 else 1, first + col + 1, z + 1))
                        else:
                            tiles.append(tile_at(vol, first + col + 1, 8 if b == 0 else 1, z + 1))
                tiles.append(msg[first * 64 : (first + 2) * 64])
                parts.append(jnp.concatenate(tiles, axis=0))
            data = jnp.concatenate(parts, axis=1)
            out = jnp.dot(sel[0:320, :], data, preferred_element_type=F32).astype(BF)
            for k in range(2):
                for zp in range(10):
                    for col in range(2):
                        at = (half * 2 + k) * 2 + col + 1
                        row = (zp * 2 + col) * SLOTS
                        value = out[row : row + SLOTS, k * 128 : (k + 1) * 128]
                        if b == 1:
                            put_tile(vol, 0 if a == 0 else 9, at, zp, value)
                        else:
                            put_tile(vol, at, 0 if b == 0 else 9, zp, value)

    for c in (0, 2):
        for v in range(16):
            rows = pl.ds(v * SLOTS, SLOTS)
            j = v // 8
            want = base + (tap_delta(1, 1, c) + VSTEP * v)
            sel[rows, j * 128 : (j + 1) * 128] = one_hot(want, own + VSTEP * 8 * j)
            sel[rows, (1 - j) * 128 : (2 - j) * 128] = nothing
        for half in range(2):
            parts = []
            for k in range(2):
                tiles = []
                for v in range(16):
                    at = (half * 2 + k) * 16 + v
                    tiles.append(tile_at(vol, at // 8 + 1, at % 8 + 1, 8 if c == 0 else 1))
                parts.append(jnp.concatenate(tiles, axis=0))
            data = jnp.concatenate(parts, axis=1)
            out = jnp.dot(sel[0:256, 0:256], data, preferred_element_type=F32).astype(BF)
            for k in range(2):
                for v in range(16):
                    at = (half * 2 + k) * 16 + v
                    put_tile(
                        vol,
                        at // 8 + 1,
                        at % 8 + 1,
                        0 if c == 0 else 9,
                        out[v * SLOTS : (v + 1) * SLOTS, k * 128 : (k + 1) * 128],
                    )

    for a in (0, 2):
        for b in (0, 2):
            side = left if a == 0 else right
            face = lower if b == 0 else upper
            side_code = label_code(side[FACE : FACE + 1], a - 1, 0)
            face_code = label_code(face[FACE : FACE + 1], 0, b - 1)
            corner_at = XMSG if a == 0 else XMSG + 64
            corner_lab = XMSG + 128 if a == 0 else XMSG + 128 + LAB
            corner_code = label_code(face[corner_lab : corner_lab + 1], a - 1, b - 1)
            voxel = VSTEP * (lane % 64 // BORDER)
            beside = jnp.where(lane < 64, side_code, face_code) + voxel
            across = jnp.where(lane < 64, corner_code, NOWHERE) + voxel
            for zp in range(10):
                rows = pl.ds(zp * SLOTS, SLOTS)
                want = base + (tap_delta(a, b, cs[zp]) + VSTEP * zs[zp])
                sel[rows, 0:128] = one_hot(want, own)
                sel[rows, 128:256] = one_hot(want, beside)
                sel[rows, 256:384] = one_hot(want, across)
            xs = 8 if a == 0 else 1
            ys = 8 if b == 0 else 1
            tiles = [tile_at(vol, xs, ys, z + 1) for z in range(8)]
            line_y = (7 if b == 0 else 0) * 64
            line_x = (7 if a == 0 else 0) * 64
            tiles.append(side[line_y : line_y + 64])
            tiles.append(face[line_x : line_x + 64])
            tiles.append(face[corner_at : corner_at + 64])
            tiles.append(jnp.zeros((64, CH), BF))
            data = jnp.concatenate(tiles, axis=0)
            out = jnp.dot(sel[0:160, :], data, preferred_element_type=F32).astype(BF)
            for zp in range(10):
                put_tile(
                    vol,
                    0 if a == 0 else 9,
                    0 if b == 0 else 9,
                    zp,
                    out[zp * SLOTS : (zp + 1) * SLOTS],
                )


def pair_weights(wide, block):
    zero = jnp.zeros((CH, CH), BF)
    for a in range(3):
        for b in range(3):
            w0, w1, w2 = (block(a, b, c) for c in range(3))
            k = (a * 3 + b) * 2
            wide[k * 256 : k * 256 + 128, 0:128] = w0
            wide[k * 256 : k * 256 + 128, 128:256] = zero
            wide[k * 256 + 128 : k * 256 + 256, 0:128] = w1
            wide[k * 256 + 128 : k * 256 + 256, 128:256] = w0
            wide[k * 256 + 256 : k * 256 + 384, 0:128] = w2
            wide[k * 256 + 256 : k * 256 + 384, 128:256] = w1
            wide[k * 256 + 384 : k * 256 + 512, 0:128] = zero
            wide[k * 256 + 384 : k * 256 + 512, 128:256] = w2


def window(vol, x0, nx, a, b, h):
    return vol[pl.ds(x0 + a, nx), b : b + EDGE, h : h + 4].reshape(nx * EDGE * 4 * SLOTS, 256)


def conv_rows(vol, wide, x0, nx):
    taps = [window(vol, x0, nx, k // 6, k // 2 % 3, k % 2) for k in range(18)]
    return jnp.dot(jnp.concatenate(taps, axis=1), wide[...], preferred_element_type=F32)


def slot_values(coord, count, routes):
    sub = lax.broadcasted_iota(jnp.int32, (SLOTS, 128), 0)
    lane = lane_row()
    base = jnp.zeros((SLOTS, 128), jnp.int32)
    target = jnp.full((SLOTS, 128), NOWHERE, jnp.int32)
    own = jnp.full((1, 128), NOWHERE, jnp.int32)
    target_row = jnp.full((1, 128), NOWHERE, jnp.int32)
    for s in range(SLOTS):
        x, y, z = (coord[d, s] for d in range(3))
        live = (s if s < BORDER else s - BORDER) < count[0, 0, 0 if s < BORDER else 1]
        code = position_code(x, y, z)
        place = jnp.where(live, routes[0, s] * CAP + routes[1, s], NOWHERE)
        base = jnp.where(sub == s, code, base)
        target = jnp.where(sub == s, place, target)
        own = jnp.where(lane % SLOTS == s, jnp.where(live, code, NOWHERE), own)
        target_row = jnp.where(lane % SLOTS == s, place, target_row)
    return base, target, own, target_row


def put_labels(coord, count, faces):
    lane = lane_row()
    row = jnp.zeros((1, 128), jnp.int32)
    for s in range(BORDER):
        x, y, z = (coord[d, s] for d in range(3))
        label = jnp.where(s < count[0, 0, 0], 1 + x + TILE * y + TILE * TILE * z, 0)
        row = jnp.where(lane % BORDER == s, label, row)
    rows = jnp.broadcast_to(row.astype(F32), (LAB, 128)).astype(BF)
    for face in faces:
        face[FACE:XMSG] = rows


def occupied_lanes(count, slots, lane_slot):
    live = (lane_slot < BORDER) & (lane_slot < count[0, 0, 0])
    live = live | ((lane_slot >= BORDER) & (lane_slot - BORDER < count[0, 0, 1]))
    return jnp.where(live, 1.0, 0.0).astype(BF)


def put_faces(vol, xlo, xhi, ylo, yhi):
    r = lax.broadcasted_iota(jnp.int32, (128, 256), 0)
    k = lax.broadcasted_iota(jnp.int32, (128, 256), 1)
    chosen = one_hot(r // BORDER * SLOTS + r % BORDER, k)
    for face, at, along_y in ((xlo, 1, True), (xhi, 8, True), (ylo, 1, False), (yhi, 8, False)):
        for q in range(4):
            tiles = []
            for col in range(2):
                line = 2 * q + col + 1
                for z in range(8):
                    place = (at, line) if along_y else (line, at)
                    tiles.append(tile_at(vol, *place, z + 1))
            data = jnp.concatenate(tiles, axis=0)
            out = jnp.dot(chosen, data, preferred_element_type=F32)
            face[q * 128 : (q + 1) * 128] = out.astype(BF)


def faces_kernel(feats, mask_rows, coord, count, xlo, xhi, ylo, yhi):
    r = lax.broadcasted_iota(jnp.int32, (128, 128), 0)
    k = lax.broadcasted_iota(jnp.int32, (128, 128), 1)
    order = one_hot((r % BORDER) * 16 + r // BORDER, k)
    order = order * occupied_lanes(count, BORDER, lane_row() // 16)

    def rows(x, q, first, last):
        data = feats[:, x * 64 + q * 16 : x * 64 + (q + 1) * 16, :].reshape(128, CH)
        chosen = order[first:last] * mask_rows[x, q : q + 1, 0:128]
        return jnp.dot(chosen, data, preferred_element_type=F32).astype(BF)

    for q in range(4):
        xlo[q * 128 : (q + 1) * 128] = rows(0, q, 0, 128)
        xhi[q * 128 : (q + 1) * 128] = rows(EDGE - 1, q, 0, 128)
    for x in range(EDGE):
        ylo[x * 64 : (x + 1) * 64] = rows(x, 0, 0, 64)
        yhi[x * 64 : (x + 1) * 64] = rows(x, 3, 64, 128)
    put_labels(coord, count, (xlo, xhi, ylo, yhi))


def arrange(feats, mask_rows, count, vol, mask):
    r = lax.broadcasted_iota(jnp.int32, (256, 256), 0)
    k = lax.broadcasted_iota(jnp.int32, (256, 256), 1)
    order = one_hot((r % SLOTS) * 16 + r // SLOTS, k)
    order = order * occupied_lanes(
        count, SLOTS, lax.broadcasted_iota(jnp.int32, (1, 256), 1) // 16
    )
    ones = jnp.ones((256, CH), BF)

    def at_x(x, carry):
        for q in range(4):
            first = pl.multiple_of(x * 64 + q * 16, 16)
            data = feats[:, pl.ds(first, 16), :].reshape(256, CH)
            chosen = order * mask_rows[x, q : q + 1, :]
            out = jnp.dot(
                chosen, jnp.concatenate([data, ones], axis=1), preferred_element_type=F32
            )
            tiles = out.astype(BF).reshape(2, 8, SLOTS, 256)
            for y in range(2):
                for z in range(8):
                    put_tile(vol, x + 1, q * 2 + y + 1, z + 1, tiles[y, z, :, 0:CH])
                    mask[x, q * 2 + y, z // 2, :, (z % 2) * CH : (z % 2 + 1) * CH] = tiles[
                        y, z, :, CH : 2 * CH
                    ]
        return carry

    lax.fori_loop(0, EDGE, at_x, 0)


def forward_kernel(
    feats, mask_rows, left, right, lower, upper, coord, count, routes, weight, down, returned,
    grad_out, gxlo, gxhi, gylo, gyhi, sending, partial,
    vol, sel, wide, grad_t, route, spread, acts, subs, mask, grad_vol, sem,
):
    base, target, own, target_row = slot_values(coord, count, routes)
    pair_weights(wide, lambda a, b, c: weight[((a * 3 + b) * 3 + c) * CH :][:CH])
    arrange(feats, mask_rows, count, vol, mask)
    fill_halo(vol, sel, base, own, left, right, lower, upper)

    lane = lane_row()
    for b in range(16):
        for j in range(4):
            route[b * 16 : (b + 1) * 16, j * 128 : (j + 1) * 128] = one_hot(
                target * 16 + b, lane + 128 * j
            )
    block = lax.broadcasted_iota(jnp.int32, (16, 128), 0)
    for t in range(2 * SLOTS):
        for j in range(2):
            spread[t * 16 : (t + 1) * 16, j * 128 : (j + 1) * 128] = one_hot(
                block * 64 + t, target_row + 64 * (lane // 16 + 8 * j)
            )

    def at_hx(hx, carry):
        pre_all = conv_rows(vol, wide, 2 * hx, 2).reshape(2, 4, 2, 64, 256)
        first = pl.multiple_of(hx * 16, 16)
        grad_sub = jnp.dot(
            route[...],
            returned[:, pl.ds(first, 16), :].reshape(512, CH),
            preferred_element_type=F32,
        ).astype(BF)
        subs[pl.ds(pl.multiple_of(hx * 256, 256), 256)] = grad_sub
        grad_act = lax.dot_general(
            grad_sub, down[...], (((1,), (1,)), ((), ())), preferred_element_type=F32
        )
        total = None
        for px in range(2):
            for py in range(2):
                q = px * 2 + py
                x = 2 * hx + px
                pre = pre_all[px, :, py].reshape(256, 256)
                live = jnp.stack([mask[x, 2 * hy + py] for hy in range(4)]).reshape(256, 256)
                live = live.astype(F32)
                sig = jax.nn.sigmoid(pre)
                act = (pre * sig * live).astype(BF)
                acts[q, pl.ds(pl.multiple_of(hx * 256, 256), 256)] = act
                term = jnp.dot(
                    act, down[q * 256 : (q + 1) * 256], preferred_element_type=F32
                )
                total = term if total is None else total + term
                grad = (
                    grad_act[:, q * 256 : (q + 1) * 256]
                    * live
                    * sig
                    * (1.0 + pre * (1.0 - sig))
                )
                grad_b = grad.astype(BF)
                shaped = grad_b.reshape(4, 4, SLOTS, 256)
                turned = grad_b.T
                for hy in range(4):
                    y = 2 * hy + py
                    for p in range(4):
                        put_tile(grad_vol, x + 1, y + 1, 2 * p + 1, shaped[hy, p, :, 0:CH])
                        put_tile(grad_vol, x + 1, y + 1, 2 * p + 2, shaped[hy, p, :, CH:256])
                grad_t[hx, q] = turned
        sub = total.astype(BF)
        sent = jnp.dot(spread[...], sub, preferred_element_type=F32).astype(BF)
        sending[:, pl.ds(first, 16), :] = sent.reshape(2 * SLOTS, 16, CH)
        return carry

    lax.fori_loop(0, EDGE // 2, at_hx, 0)
    copy = pltpu.make_async_copy(grad_vol, grad_out, sem)
    copy.start()
    put_faces(grad_vol, gxlo, gxhi, gylo, gyhi)
    put_labels(coord, count, (gxlo, gxhi, gylo, gyhi))

    subs_t = subs[...].T
    for q in range(4):
        found = jnp.dot(subs_t, acts[q], preferred_element_type=F32)
        partial[3456 + q * 256 : 3456 + (q + 1) * 256] = found.T.astype(BF)

    for ab in range(9):
        a, b = ab // 3, ab % 3
        halves = []
        for h in range(2):
            total = None
            for hx in range(4):
                for q in range(4):
                    px, py = q // 2, q % 2
                    rows = jnp.stack(
                        [
                            vol[2 * hx + px + a, 2 * hy + py + b, h : h + 4]
                            for hy in range(4)
                        ]
                    ).reshape(256, 256)
                    term = jnp.dot(grad_t[hx, q], rows, preferred_element_type=F32)
                    total = term if total is None else total + term
            halves.append(total)
        low, high = halves
        taps = [
            low[0:128, 0:128] + low[128:256, 128:256],
            low[0:128, 128:256] + high[128:256, 0:128],
            high[0:128, 0:128] + high[128:256, 128:256],
        ]
        for c in range(3):
            row = (ab * 3 + c) * CH
            partial[row : row + CH] = taps[c].T.astype(BF)
    partial[4480:] = jnp.zeros((SHARD * 128 - 4480, CH), BF)
    copy.wait()


def backward_kernel(
    grad_in, mask_rows, left, right, lower, upper, coord, count, routes, weight,
    feat_grad, vol, sel, wide, sem,
):
    copy = pltpu.make_async_copy(grad_in, vol, sem)
    copy.start()
    base, _, own, _ = slot_values(coord, count, routes)
    pair_weights(
        wide, lambda a, b, c: weight[((2 - a) * 9 + (2 - b) * 3 + 2 - c) * CH :][:CH].T
    )
    copy.wait()
    fill_halo(vol, sel, base, own, left, right, lower, upper)
    r = lax.broadcasted_iota(jnp.int32, (256, 256), 0)
    k = lax.broadcasted_iota(jnp.int32, (256, 256), 1)
    order = one_hot(
        (r % 2) * 128 + (r // 8 % 2) * 64 + (r // 2 % 4) * 16 + r // 16, k
    )
    order = order * occupied_lanes(
        count, SLOTS, lax.broadcasted_iota(jnp.int32, (1, 256), 1) % SLOTS
    )

    def at_hx(hx, carry):
        back = conv_rows(vol, wide, 2 * hx, 2).astype(BF).reshape(2, 4, 128, 256)
        for px in range(2):
            for q in range(4):
                x = 2 * hx + px
                data = jnp.concatenate(
                    [back[px, q, :, 0:CH], back[px, q, :, CH:256]], axis=0
                )
                chosen = order * mask_rows[x, q : q + 1, :]
                out = jnp.dot(chosen, data, preferred_element_type=F32).astype(BF)
                first = pl.multiple_of(x * 64 + q * 16, 16)
                feat_grad[:, pl.ds(first, 16), :] = out.reshape(SLOTS, 16, CH)
        return carry

    lax.fori_loop(0, EDGE // 2, at_hx, 0)


def later_kernel(value, after, same):
    same[...] = value[...]


VMEM_LIMIT = 56 * 1024 * 1024
VOLUME = (10, 10, 5, SLOTS, 256)


def whole(count):
    return [pl.BlockSpec(memory_space=pltpu.VMEM)] * count


def scalar(count):
    return [pl.BlockSpec(memory_space=pltpu.SMEM)] * count


def microseconds(time):
    return pl.CostEstimate(flops=int(time * 1.1e9), bytes_accessed=1 << 20, transcendentals=0)


def shift(value, axis, step):
    count = lax.axis_size(axis)
    if step > 0:
        pairs = [(i, i + 1) for i in range(count - 1)]
    else:
        pairs = [(i + 1, i) for i in range(count - 1)]
    return lax.ppermute(value, axis, pairs)


def exchange(xlo, xhi, ylo, yhi):
    left = shift(xhi, "gx", 1)
    right = shift(xlo, "gx", -1)
    ends = [left[FACE:XMSG], right[FACE:XMSG]]
    up = jnp.concatenate([yhi, left[FACE - 64 : FACE], right[FACE - 64 : FACE]] + ends)
    down = jnp.concatenate([ylo, left[0:64], right[0:64]] + ends)
    lower = shift(up, "gy", 1)
    upper = shift(down, "gy", -1)
    return left, right, lower, upper


def per_device(
    feats, voxel_mask, brick_coord, brick_count, route, conv_weight, down_weight, coarse_grad
):
    tiles_x = lax.axis_size("gx")
    tiles_y = lax.axis_size("gy")
    devices = tiles_x * tiles_y
    active = voxel_mask[0, 0].astype(BF)
    mask_rows = active.reshape(SLOTS, EDGE, 4, 16).transpose(1, 2, 0, 3).reshape(EDGE, 4, 256)
    by_pair = active.reshape(SLOTS, EDGE, 4, 2, 4, 2)
    back_rows = by_pair.transpose(1, 2, 5, 3, 4, 0).reshape(EDGE, 4, 256)
    scalars = (brick_coord[0, 0].T, brick_count, route[0, 0].T)

    face = jax.ShapeDtypeStruct((XMSG, CH), BF)
    volume = jax.ShapeDtypeStruct(VOLUME, BF)
    faces = pl.pallas_call(
        faces_kernel,
        grid=(1,),
        out_shape=(face,) * 4,
        in_specs=[pl.BlockSpec((BORDER, VOX, CH), lambda i: (0, 0, 0))] + whole(1) + scalar(2),
        out_specs=tuple(whole(4)),
        compiler_params=pltpu.CompilerParams(vmem_limit_bytes=VMEM_LIMIT),
        cost_estimate=microseconds(2),
        name="faces",
    )(feats[0, 0], mask_rows, *scalars[:2])
    around = exchange(*faces)
    cotangents = pl.pallas_call(
        later_kernel,
        out_shape=jax.ShapeDtypeStruct((tiles_x, CAP * 64, CH), BF),
        in_specs=whole(2),
        out_specs=whole(1)[0],
        compiler_params=pltpu.CompilerParams(vmem_limit_bytes=VMEM_LIMIT),
        cost_estimate=microseconds(1),
        name="later",
    )(coarse_grad[0, 0].reshape(tiles_x, CAP * 64, CH), around[0])
    returned = lax.all_to_all(
        cotangents, "gx", 0, 0, tiled=True
    ).reshape(2 * SLOTS, 64, CH)

    grad_vol, gxlo, gxhi, gylo, gyhi, sending, partial = pl.pallas_call(
        forward_kernel,
        out_shape=(volume,)
        + (face,) * 4
        + (
            jax.ShapeDtypeStruct((2 * SLOTS, 64, CH), BF),
            jax.ShapeDtypeStruct((SHARD * 128, CH), BF),
        ),
        in_specs=whole(6) + scalar(3) + whole(3),
        out_specs=(pl.BlockSpec(memory_space=pl.ANY),) + tuple(whole(6)),
        scratch_shapes=[
            pltpu.VMEM(VOLUME, BF),
            pltpu.VMEM((320, 384), BF),
            pltpu.VMEM((18 * 256, 256), BF),
            pltpu.VMEM((4, 4, 256, 256), BF),
            pltpu.VMEM((256, 512), BF),
            pltpu.VMEM((512, 256), BF),
            pltpu.VMEM((4, 1024, 256), BF),
            pltpu.VMEM((1024, CH), BF),
            pltpu.VMEM((8, 8, 4, SLOTS, 256), BF),
            pltpu.VMEM(VOLUME, BF),
            pltpu.SemaphoreType.DMA(()),
        ],
        compiler_params=pltpu.CompilerParams(vmem_limit_bytes=VMEM_LIMIT),
        cost_estimate=microseconds(34),
        name="forward",
    )(feats[0, 0], mask_rows, *around, *scalars, conv_weight, down_weight, returned)

    around = exchange(gxlo, gxhi, gylo, gyhi)
    shares = tiles_x * SHARD
    parts = lax.all_to_all(partial.reshape(tiles_y, shares, CH), "gy", 0, 0, tiled=True)
    feat_grad = pl.pallas_call(
        backward_kernel,
        out_shape=jax.ShapeDtypeStruct((SLOTS, VOX, CH), BF),
        in_specs=[pl.BlockSpec(memory_space=pl.ANY)]
        + whole(5)
        + scalar(3)
        + whole(1),
        out_specs=whole(1)[0],
        scratch_shapes=[
            pltpu.VMEM(VOLUME, BF),
            pltpu.VMEM((320, 384), BF),
            pltpu.VMEM((18 * 256, 256), BF),
            pltpu.SemaphoreType.DMA(()),
        ],
        compiler_params=pltpu.CompilerParams(vmem_limit_bytes=VMEM_LIMIT),
        cost_estimate=microseconds(18),
        name="backward",
    )(grad_vol, back_rows, *around, *scalars, conv_weight)

    total = jnp.sum(parts.astype(F32), axis=0).astype(BF).reshape(tiles_x, SHARD, CH)
    message = jnp.concatenate([sending.reshape(tiles_x, CAP * 64, CH), total], axis=1)
    parts = lax.all_to_all(message, "gx", 0, 0, tiled=True)
    coarse = parts[:, : CAP * 64].reshape(1, 1, 2 * SLOTS, 64, CH)
    total = jnp.sum(parts[:, CAP * 64 :].astype(F32), axis=0).astype(BF)
    sums = lax.all_to_all(
        jnp.broadcast_to(total[None], (devices, SHARD, CH)), ("gy", "gx"), 0, 0, tiled=True
    ).reshape(devices * SHARD, CH)
    total_slots = devices * SLOTS
    conv_grad = sums[:3456].astype(F32) * (1.0 / math.sqrt(total_slots * VOX))
    down_grad = sums[3456:4480].astype(F32) * (1.0 / math.sqrt(total_slots * VOX // 8))
    return (coarse, feat_grad[None, None], conv_grad, down_grad)


def solution(mesh):
    in_specs = (
        P("gx", "gy", None, None, None),
        P("gx", "gy", None, None),
        P("gx", "gy", None, None),
        P("gx", "gy", None),
        P("gx", "gy", None, None),
        P(),
        P(),
        P("gx", "gy", None, None, None),
    )
    out_specs = (P("gx", "gy", None, None, None), P("gx", "gy", None, None, None), P(), P())
    return jax.shard_map(
        per_device, mesh=mesh, in_specs=in_specs, out_specs=out_specs, check_vma=False
    )
```
